512 devices in a mesh: slab: 16 (over y, core), sub: 32 (over z, x).
Axes of the slice: x: 4, y: 8, z: 8, core: 2. Of those that a mesh axis runs over, the one named last changes fastest.
Arguments:
- positions: float32 [3, 8192, 256], P(None, ('slab', 'sub')), may hold values from 0 to 1
- velocities: float32 [3, 8192, 256], P(None, ('slab', 'sub')), may hold values from -6 to 6
- mass: float32 [8192, 256], P(('slab', 'sub')), may hold values from 0.0001953125 to 0.0009765625
- smoothing: float32 [8192, 256], P(('slab', 'sub')), may hold values from 0.08 to 0.15
- energy: float32 [8192, 256], P(('slab', 'sub')), may hold values from 0.2 to 2
- cell_counts: int32 [8192], P(('slab', 'sub')), may hold values from 128 to 256, as said below
- send_cells: int32 [512, 32, 2], P(('slab', 'sub')), may hold values from 0 to 15, as said below
- partners: int32 [8192, 8], P(('slab', 'sub')), may hold values from 0 to 81, as said below
- mig_list: int32 [512, 32, 8], P(('slab', 'sub')), may hold values from 0 to 4095, as said below
- mig_counts: int32 [512, 32], P(('slab', 'sub')), may hold values from 1 to 8, as said below
Outputs:
- density: float32 [8192, 256], P(('slab', 'sub'))
- state: float32 [6, 8192, 256], P(None, ('slab', 'sub'))
- arrivals: float32 [6, 131072], P(None, ('slab', 'sub'))
The draws below stay inside these ranges and needn't reach their ends.
Inputs may be any that keep to these rules, and one draw needn't show every extreme that they name: `cell_counts`: every cell has at least half of its slots live; the first cell holds 256. `send_cells`: the 2 cells sent to one device are distinct. `partners`: a row is distinct indices; its first is the cell itself (1 plus its index within the device), its second a lower rim cell for the first half of a device's cells and an upper rim cell for the second half. `mig_list`: every entry names a live slot. `mig_counts`: each device sends 8 to some device of its slab, and in each slab one device receives 8 from every sender.
All inputs are finite; a program needn't handle non-finite values.
Results may differ from the reference program's by a relative error of at most 0.0003.
Values sent between devices are 32-bit elements; how exact they have to be, the bound alone decides.
No kernel may reach another device: no remote copies, remote signals or barrier semaphores. Data moves between devices by JAX's collectives and lax.ppermute only.
A program may use at most 64 MiB of HBM per device.

```python
import math
import jax
import jax.numpy as jnp
from jax import lax

P_SIZE = 256
CELLS_DEV = 16
NPAIR = 8
K = 2
HB = 1
M = 8
CELLS = 8192
N_SLAB = 16
N_SUB = 32


def count_table(key):
    drawn = jax.random.randint(key, (CELLS_DEV * N_SLAB * N_SUB,), P_SIZE // 2, P_SIZE + 1)
    return jnp.where(jnp.arange(drawn.shape[0]) == 0, P_SIZE, drawn).astype(jnp.int32)


def draw_cell_counts(key, part):
    return count_table(key)


def draw_send_cells(key, part):
    key = jax.random.fold_in(key, 3)
    scores = jax.random.randint(key, (N_SLAB * N_SUB, N_SUB, CELLS_DEV), 0, 65536) * CELLS_DEV + jnp.arange(CELLS_DEV)
    return jnp.argsort(scores, axis=-1)[..., :K].astype(jnp.int32)


def draw_partners(key, part):
    key = jax.random.fold_in(key, 5)
    width = 2 * HB + CELLS_DEV + N_SUB * K
    total = CELLS_DEV * N_SLAB * N_SUB
    local = jnp.arange(total) % CELLS_DEV
    own = HB + local
    rim = jnp.where(local < CELLS_DEV // 2, local % HB, HB + CELLS_DEV + local % HB)
    slots = jnp.arange(width)[None, :]
    scores = jax.random.randint(key, (total, width), 0, 65536) * width + slots
    taken = (slots == own[:, None]) | (slots == rim[:, None])
    scores = jnp.where(taken, 2 ** 30, scores)
    others = jnp.argsort(scores, axis=-1)[:, :NPAIR - 2]
    return jnp.concatenate([own[:, None], rim[:, None], others], axis=1).astype(jnp.int32)


def draw_mig_list(key, part):
    counts = count_table(key)
    key = jax.random.fold_in(key, 7)
    first, second = jax.random.split(key)
    shape = (N_SLAB * N_SUB, N_SUB, M)
    chosen = jax.random.randint(first, shape, 0, CELLS_DEV)
    device_ids = jnp.arange(N_SLAB * N_SUB)[:, None, None]
    limit = counts[device_ids * CELLS_DEV + chosen]
    within = jax.random.randint(second, shape, 0, 1 << 20) % limit
    return (chosen * P_SIZE + within).astype(jnp.int32)


def draw_mig_counts(key, part):
    key = jax.random.fold_in(key, 11)
    first, second, third = jax.random.split(key, 3)
    senders = N_SLAB * N_SUB
    counts = jax.random.randint(first, (senders, N_SUB), 1, M + 1)
    column = jax.random.randint(second, (senders, 1), 0, N_SUB)
    target = jax.random.randint(third, (N_SLAB, 1), 0, N_SUB)
    target_rows = jnp.repeat(target, N_SUB, axis=0)
    peer_ids = jnp.arange(N_SUB)[None, :]
    counts = jnp.where((peer_ids == column) | (peer_ids == target_rows), M, counts)
    return counts.astype(jnp.int32)


def steps_of(stream_key, extent, cuts, low, high):
    loudness = 1.0
    for axis_at, shards_of in cuts:
        draws = jax.random.uniform(jax.random.fold_in(jax.random.fold_in(stream_key, 6), axis_at), (shards_of,), jnp.float32, low / len(cuts), high / len(cuts))
        loudness = loudness * jnp.repeat(jnp.exp(draws), extent[axis_at] // shards_of).reshape((-1,) + (1,) * (len(extent) - 1 - axis_at))
    return loudness


def scatter_about(key, extent, scale, reach, cuts=(), kind=jnp.bfloat16):
    factor_of = steps_of(key, extent, cuts, -0.22, 0.18) if cuts else 1.0
    entries = jax.random.normal(key, extent, jnp.float32) * scale * factor_of
    return jnp.minimum(jnp.maximum(entries, -reach), reach).astype(kind)


def setup_inputs(seed: int = 0) -> dict:
    key_of = jax.random.split(jax.random.key(seed), 11)
    return {
        "positions": jnp.clip(1.0 * jax.random.uniform(key_of[0], (3, CELLS, P_SIZE), jnp.float32) ** steps_of(key_of[0], (3, CELLS, P_SIZE), ((1, 512),), -0.2, 0.2), 0.0, 1.0),
        "velocities": scatter_about(key_of[1], (3, CELLS, P_SIZE), 1.0, 6.0, ((1, 512),), jnp.float32),
        "mass": jnp.clip(jnp.exp(math.log(0.0009765625) - 1.609438 * jax.random.uniform(key_of[2], (CELLS, P_SIZE), jnp.float32) ** steps_of(key_of[2], (CELLS, P_SIZE), ((0, 512),), -0.2, 0.2)), 0.0001953125, 0.0009765625),
        "smoothing": jnp.clip(jnp.exp(math.log(0.15) - 0.6286087 * jax.random.uniform(key_of[3], (CELLS, P_SIZE), jnp.float32) ** steps_of(key_of[3], (CELLS, P_SIZE), ((0, 512),), -0.2, 0.2)), 0.08, 0.15),
        "energy": jnp.clip(jnp.exp(math.log(2.0) - 2.3025851 * jax.random.uniform(key_of[4], (CELLS, P_SIZE), jnp.float32) ** steps_of(key_of[4], (CELLS, P_SIZE), ((0, 512),), -0.2, 0.2)), 0.2, 2.0),
        "cell_counts": draw_cell_counts(jax.random.fold_in(key_of[10], 71), 0),
        "send_cells": draw_send_cells(jax.random.fold_in(key_of[10], 71), 0),
        "partners": draw_partners(jax.random.fold_in(key_of[10], 71), 0),
        "mig_list": draw_mig_list(jax.random.fold_in(key_of[10], 71), 0),
        "mig_counts": draw_mig_counts(jax.random.fold_in(key_of[10], 71), 0),
    }


adiabatic = 5.0 / 3.0
time_step = 0.05

def separation(own_pos, others):
    apart_x = own_pos[0][:, None] - others[0][None, :]
    apart_y = own_pos[1][:, None] - others[1][None, :]
    apart_z = own_pos[2][:, None] - others[2][None, :]
    radius = jnp.sqrt(apart_x * apart_x + apart_y * apart_y + apart_z * apart_z)
    return (apart_x, apart_y, apart_z, radius)

def pair_density(own_pos, own_width, nearby):
    others = nearby[:3].reshape(3, -1)
    masses = nearby[3].reshape(-1)
    apart_x, apart_y, apart_z, radius = separation(own_pos, others)
    scaled = radius / own_width[:, None]
    inside = 1.0 - 1.5 * scaled * scaled + 0.75 * scaled * scaled * scaled
    remain = jnp.maximum(2.0 - scaled, 0.0)
    kernel = jnp.where(scaled < 1.0, inside, 0.25 * remain * remain * remain)
    return lax.optimization_barrier(jnp.sum(kernel * masses[None, :], axis=1)) / (math.pi * own_width ** 3)

def pair_force(own_pos, own_width, own_press, nearby):
    others = nearby[:3].reshape(3, -1)
    masses = nearby[3].reshape(-1)
    press = nearby[4].reshape(-1)
    apart_x, apart_y, apart_z, radius = separation(own_pos, others)
    scaled = radius / own_width[:, None]
    remain = jnp.maximum(2.0 - scaled, 0.0)
    slope = jnp.where(scaled < 1.0, -3.0 + 2.25 * scaled, -0.75 * remain * remain / jnp.maximum(scaled, 1.0))
    factor = masses[None, :] * (own_press[:, None] + press[None, :]) * slope
    push = jnp.stack([lax.optimization_barrier(jnp.sum(factor * apart_x, axis=1)), lax.optimization_barrier(jnp.sum(factor * apart_y, axis=1)), lax.optimization_barrier(jnp.sum(factor * apart_z, axis=1))])
    return -push / (math.pi * own_width ** 5)

def density_cell(items):
    return pair_density(items[0], items[1], items[2])

def force_cell(items):
    return pair_force(items[0], items[1], items[2], items[3])

def build_table(source, send_cells):
    devices = N_SLAB * N_SUB
    device_ids = jnp.arange(devices)
    slab_id = device_ids // N_SUB
    sub_id = device_ids % N_SUB
    lower_rim = source[(slab_id - 1) % N_SLAB * N_SUB + sub_id][:, CELLS_DEV - HB:]
    upper_rim = source[(slab_id + 1) % N_SLAB * N_SUB + sub_id][:, :HB]
    senders = slab_id[:, None] * N_SUB + jnp.arange(N_SUB)[None, :]
    listed = send_cells[senders, sub_id[:, None]]
    proxies = source[senders[:, :, None], listed]
    proxies = proxies.reshape(devices, N_SUB * K, source.shape[2], P_SIZE)
    return jnp.concatenate([lower_rim, source, upper_rim, proxies], axis=1)

def reference(positions, velocities, mass, smoothing, energy, cell_counts, send_cells, partners, mig_list, mig_counts):
    devices = N_SLAB * N_SUB
    total = devices * CELLS_DEV
    valid = jnp.arange(P_SIZE)[None, :] < cell_counts[:, None]
    mass_live = jnp.where(valid, mass, 0.0)
    block = jnp.concatenate([positions, mass_live[None]], axis=0)
    source = block.reshape(4, devices, CELLS_DEV, P_SIZE).transpose(1, 2, 0, 3)
    table = build_table(source, send_cells)
    device_ids = jnp.arange(devices)[:, None, None]
    links = partners.reshape(devices, CELLS_DEV, NPAIR)
    nearby = table[device_ids, links].reshape(total, NPAIR, 4, P_SIZE).transpose(0, 2, 1, 3)
    own_pos = positions.transpose(1, 0, 2)
    density = lax.map(density_cell, (own_pos, smoothing, nearby))
    pressure = jnp.where(valid, (adiabatic - 1.0) * energy / jnp.where(valid, density, 1.0), 0.0)
    press_table = build_table(pressure.reshape(devices, CELLS_DEV, 1, P_SIZE), send_cells)
    full = jnp.concatenate([table, press_table], axis=2)
    nearby_all = full[device_ids, links].reshape(total, NPAIR, 5, P_SIZE).transpose(0, 2, 1, 3)
    push = lax.map(force_cell, (own_pos, smoothing, pressure, nearby_all))
    velocity = velocities + time_step * push.transpose(1, 0, 2)
    place = positions + time_step * velocity
    state = jnp.where(valid[None], jnp.concatenate([place, velocity], axis=0), 0.0)
    flat = state.reshape(6, devices, CELLS_DEV * P_SIZE).transpose(1, 2, 0)
    picked = flat[jnp.arange(devices)[:, None, None], mig_list]
    picked = picked.reshape(N_SLAB, N_SUB, N_SUB, M, 6).transpose(0, 2, 1, 3, 4)
    counts = mig_counts.reshape(N_SLAB, N_SUB, N_SUB).transpose(0, 2, 1)
    keep = jnp.arange(M)[None, None, None, :] < counts[..., None]
    picked = jnp.where(keep[..., None], picked, 0.0)
    arrivals = picked.transpose(4, 0, 1, 2, 3).reshape(6, devices * N_SUB * M)
    return (jnp.where(valid, density, 0.0), state, arrivals)
```

```python
import functools
import math

import jax
import jax.numpy as jnp
from jax import lax
from jax.experimental import pallas as pl
from jax.experimental.pallas import tpu as pltpu
from jax.sharding import PartitionSpec as P

P_SIZE = 256
HALF = 128
M = 8
K_ROWS = 48
V_ROWS = 32
ROW_BLOCK = 32
SIZES = (128, 160, 192, 224, 256)
TINY = 1e-12

adiabatic = 5.0 / 3.0
time_step = 0.05

VMEM = pl.BlockSpec(memory_space=pltpu.VMEM)
SMEM = pl.BlockSpec(memory_space=pltpu.SMEM)
PARAMS = pltpu.CompilerParams(vmem_limit_bytes=56 * 1024 * 1024)


def split(value):
    high = value.astype(jnp.bfloat16).astype(jnp.float32)
    rest = value - high
    mid = rest.astype(jnp.bfloat16).astype(jnp.float32)
    return high, mid, rest - mid


def row_ids():
    return lax.broadcasted_iota(jnp.int32, (8, HALF), 0)


def half_rows(record, half):
    return record if half == 0 else pltpu.roll(record, 4, 0)


def norms(tile, row):
    square = tile * tile
    return (
        pltpu.roll(square, row, 0) + pltpu.roll(square, row - 1, 0) + pltpu.roll(square, row - 2, 0)
    )


def right_operand(record):
    rows = row_ids()
    parts = []
    for half in range(2):
        tile = half_rows(record, half)
        feature = jnp.where(rows < 4, tile, 0.0)
        feature = jnp.where(rows == 4, norms(tile, 4), feature)
        feature = jnp.where(rows == 5, 1.0, feature)
        high, mid, low = split(feature)
        parts.append(jnp.concatenate([high, high, mid, high, low, mid], axis=0))
    return jnp.concatenate(parts, axis=1).astype(jnp.bfloat16)


def left_operand(record, width):
    rows = row_ids()
    parts = []
    for half in range(2):
        tile = half_rows(record, half)
        h = width[:, half * HALF : (half + 1) * HALF]
        scale = jnp.broadcast_to(1.0 / (h * h), (8, HALF))
        feature = jnp.where(rows < 3, -2.0 * scale * tile, 0.0)
        feature = jnp.where(rows == 4, scale, feature)
        feature = jnp.where(rows == 5, scale * norms(tile, 5), feature)
        high, mid, low = split(feature)
        pad = jnp.zeros((HALF - K_ROWS, HALF), jnp.float32)
        parts.append(jnp.concatenate([high, mid, high, low, high, mid, pad], axis=0).T)
    return jnp.concatenate(parts, axis=0).astype(jnp.bfloat16)


def pack_kernel(counts, send, pos, mass, rec, out):
    cells = mass.shape[0]
    lane = lax.broadcasted_iota(jnp.int32, (1, P_SIZE), 1)
    for c in range(cells):
        live = lane < counts[c]
        for k in range(4):
            row = pos[k, c : c + 1, :] - 0.5 if k < 3 else mass[c : c + 1, :]
            row = jnp.where(live, row, 0.0)
            rec[c, k : k + 1, :] = row[:, :HALF]
            rec[c, k + 4 : k + 5, :] = row[:, HALF:]
    for v in range(out.shape[0]):
        for k in range(send.shape[0]):
            out[v, 8 * k : 8 * k + 8, :] = rec[send[k, v]]


def fill_table(rec, rim_lo, rim_hi, recv, table):
    cells = rec.shape[0]
    table[0] = rim_lo[0]
    for c in range(cells):
        table[1 + c] = rec[c]
    table[cells + 1] = rim_hi[0]
    peers = recv.shape[0]
    per_peer = recv.shape[1] // 8
    for v in range(peers):
        for k in range(per_peer):
            table[cells + 2 + v * per_peer + k] = recv[v, 8 * k : 8 * k + 8, :]


def fill_operands(table, rec, smoothing, right, left):
    def table_step(t, carry):
        right[t] = right_operand(table[t])
        return carry

    lax.fori_loop(0, table.shape[0], table_step, 0, unroll=2)
    for c in range(rec.shape[0]):
        left[c] = left_operand(rec[c], smoothing[c : c + 1, :])


def by_size(count, run):
    for k, size in enumerate(SIZES):
        below = SIZES[k - 1] if k else -1
        pl.when((count > below) & (count <= size))(functools.partial(run, size))


def density_kernel(
    counts, partners, send, rec, rim_lo, rim_hi, recv, smoothing, energy,
    density, press, press_rec, press_send,
    table, right, left, square, total,
):
    cells = rec.shape[0]
    pairs = partners.shape[0]
    fill_table(rec, rim_lo, rim_hi, recv, table)
    fill_operands(table, rec, smoothing, right, left)

    def cell(c, carry):
        def run(size):
            def product(p):
                square[p % 2, :size, :] = jnp.dot(
                    left[c, :size, :K_ROWS], right[partners[p, c]], preferred_element_type=jnp.float32
                )

            product(0)
            for p in range(pairs):
                if p + 1 < pairs:
                    product(p + 1)
                t = partners[p, c]
                masses = (table[t, 3:4, :], table[t, 7:8, :])
                for base in range(0, size, ROW_BLOCK):
                    block = pl.ds(base, ROW_BLOCK)
                    term = 0.0
                    for half in range(2):
                        s = jnp.maximum(square[p % 2, block, half * HALF : (half + 1) * HALF], TINY)
                        q = s * lax.rsqrt(s)
                        outer = jnp.maximum(2.0 - q, 0.0)
                        inner = jnp.maximum(outer - 1.0, 0.0)
                        w = 0.25 * (outer * outer * outer) - inner * inner * inner
                        term = term + w * masses[half]
                    total[c, block, :] = term if p == 0 else total[c, block, :] + term
            if size < P_SIZE:
                total[c, size:, :] = jnp.zeros((P_SIZE - size, HALF), jnp.float32)

        by_size(counts[c], run)
        return carry

    lax.fori_loop(0, cells, cell, 0)

    ones = jnp.ones((8, HALF), jnp.float32)
    lane = lax.broadcasted_iota(jnp.int32, (1, P_SIZE), 1)
    for c in range(cells):
        summed = lax.dot_general(
            ones, total[c], (((1,), (1,)), ((), ())),
            precision=lax.Precision.HIGHEST, preferred_element_type=jnp.float32,
        )[0:1, :]
        width = smoothing[c : c + 1, :]
        live = lane < counts[c]
        rho = summed / (math.pi * width * width * width)
        density[c : c + 1, :] = jnp.where(live, rho, 0.0)
        value = jnp.where(
            live, (adiabatic - 1.0) * energy[c : c + 1, :] / jnp.where(live, rho, 1.0), 0.0
        )
        press[c : c + 1, :] = value
        press_rec[c, 0:1, :] = value[:, :HALF]
        press_rec[c, 1:2, :] = value[:, HALF:]
    for v in range(send.shape[1]):
        for k in range(send.shape[0]):
            press_send[v, 2 * k : 2 * k + 2, :] = press_rec[send[k, v]]


def force_kernel(
    counts, partners, rec, rim_lo, rim_hi, recv, smoothing, press_rec, press_lo, press_hi, press_recv,
    pos, vel, press, picks,
    state, leaving,
    table, right, left, press_table, weights, square, slope_high, slope_low, total,
):
    cells = rec.shape[0]
    pairs = partners.shape[0]
    fill_table(rec, rim_lo, rim_hi, recv, table)
    fill_operands(table, rec, smoothing, right, left)
    press_table[0] = press_lo[0]
    for c in range(cells):
        press_table[1 + c] = press_rec[c]
    press_table[cells + 1] = press_hi[0]
    per_peer = press_recv.shape[1] // 2
    for v in range(press_recv.shape[0]):
        for k in range(per_peer):
            press_table[cells + 2 + v * per_peer + k] = press_recv[v, 2 * k : 2 * k + 2, :]

    def weight_step(t, carry):
        rows = row_ids()
        parts = []
        for half in range(2):
            tile = half_rows(table[t], half)
            mass = jnp.broadcast_to(tile[3:4, :], (8, HALF))
            one = jnp.where(rows == 3, 1.0, jnp.where(rows < 4, tile, 0.0))
            both = jnp.where(rows < 4, one, pltpu.roll(one, 4, 0) * press_table[t, half : half + 1, :])
            high, mid, low = split(both * mass)
            parts.append(jnp.concatenate([high, mid, low, jnp.zeros_like(low)], axis=0))
        weights[t] = jnp.concatenate(parts, axis=1).astype(jnp.bfloat16)
        return carry

    lax.fori_loop(0, table.shape[0], weight_step, 0, unroll=2)
    lane = lax.broadcasted_iota(jnp.int32, (1, P_SIZE), 1)

    def cell(c, carry):
        def run(size):
            def product(p):
                square[p % 2, :size, :] = jnp.dot(
                    left[c, :size, :K_ROWS], right[partners[p, c]], preferred_element_type=jnp.float32
                )

            def gather(p):
                w = weights[partners[p, c]]
                dims = (((1,), (1,)), ((), ()))
                added = lax.dot_general(
                    slope_high[p % 2, :size, :], w, dims, preferred_element_type=jnp.float32
                ) + lax.dot_general(
                    slope_low[p % 2, :size, :], w, dims, preferred_element_type=jnp.float32
                )
                old = total[:size, :V_ROWS]
                total[:size, :V_ROWS] = added if p == 0 else old + added

            product(0)
            for p in range(pairs):
                if p + 1 < pairs:
                    product(p + 1)
                if p:
                    gather(p - 1)
                for base in range(0, size, ROW_BLOCK):
                    block = pl.ds(base, ROW_BLOCK)
                    s = jnp.maximum(square[p % 2, block, :], TINY)
                    y = lax.rsqrt(s)
                    q = jnp.minimum(s * y, 2.0)
                    inverse = jnp.minimum(jnp.maximum(y, 0.5), 1.0)
                    f = (inverse - 1.0) + (jnp.maximum(q, 1.0) - 0.75 * q)
                    high = f.astype(jnp.bfloat16)
                    slope_high[p % 2, block, :] = high
                    slope_low[p % 2, block, :] = (f - high.astype(jnp.float32)).astype(jnp.bfloat16)
            gather(pairs - 1)

        by_size(counts[c], run)
        sums = total[...].T
        sums = sums[0:8, :] + sums[8:16, :] + sums[16:24, :]
        width = smoothing[pl.ds(c, 1), :]
        squared = width * width
        factor = (3.0 * time_step / math.pi) / (squared * squared * width)
        own = press[pl.ds(c, 1), :]
        live = lane < counts[c]
        for k in range(3):
            place = pos[k, pl.ds(c, 1), :]
            centred = place - 0.5
            push = own * (centred * sums[3:4, :] - sums[k : k + 1, :]) + (
                centred * sums[7:8, :] - sums[4 + k : 5 + k, :]
            )
            speed = vel[k, pl.ds(c, 1), :] + factor * push
            state[k, pl.ds(c, 1), :] = jnp.where(live, place + time_step * speed, 0.0)
            state[3 + k, pl.ds(c, 1), :] = jnp.where(live, speed, 0.0)
        return carry

    lax.fori_loop(0, cells, cell, 0)

    picked = picks[...]
    in_cell = picked % P_SIZE
    of_cell = picked // P_SIZE
    chosen = lax.broadcasted_iota(jnp.int32, (P_SIZE, P_SIZE), 0) == in_cell
    chosen = jnp.where(chosen, 1.0, 0.0).astype(jnp.bfloat16)
    mine = lax.broadcasted_iota(jnp.int32, (cells, P_SIZE), 0) == of_cell
    for k in range(6):
        found = 0.0
        for part in split(state[k]):
            found = found + jnp.dot(part.astype(jnp.bfloat16), chosen, preferred_element_type=jnp.float32)
        leaving[k : k + 1, :] = jnp.sum(jnp.where(mine, found, 0.0), axis=0, keepdims=True)


def neighbours(value, axis):
    count = lax.axis_size(axis)
    up = [(i, (i + 1) % count) for i in range(count)]
    down = [(j, i) for i, j in up]
    return lax.ppermute(value[-1:], axis, up), lax.ppermute(value[:1], axis, down)


def exchange(value):
    return lax.all_to_all(value, "sub", split_axis=0, concat_axis=0, tiled=True)


def on_device(
    positions, velocities, mass, smoothing, energy, cell_counts, send_cells, partners, mig_list, mig_counts
):
    cells = mass.shape[0]
    peers = lax.axis_size("sub")
    kept = send_cells.shape[2]
    width = cells + 2 + peers * kept
    f32 = jnp.float32
    send = send_cells[0].T
    links = partners.T
    rec, outgoing = pl.pallas_call(
        pack_kernel,
        out_shape=(
            jax.ShapeDtypeStruct((cells, 8, HALF), f32),
            jax.ShapeDtypeStruct((peers, 8 * kept, HALF), f32),
        ),
        in_specs=[SMEM, SMEM, VMEM, VMEM],
        out_specs=(VMEM, VMEM),
        compiler_params=PARAMS,
    )(cell_counts, send, positions, mass)
    recv = exchange(outgoing)
    rim_lo, rim_hi = neighbours(rec, "slab")

    keep = jnp.arange(M)[None, :] < mig_counts[0][:, None]
    picks = jnp.where(keep, mig_list[0], -P_SIZE).reshape(1, peers * M)

    tables = [
        pltpu.VMEM((width, 8, HALF), f32),
        pltpu.VMEM((width, K_ROWS, P_SIZE), jnp.bfloat16),
        pltpu.VMEM((cells, P_SIZE, HALF), jnp.bfloat16),
    ]
    density, press, press_rec, press_out = pl.pallas_call(
        density_kernel,
        out_shape=(
            jax.ShapeDtypeStruct((cells, P_SIZE), f32),
            jax.ShapeDtypeStruct((cells, P_SIZE), f32),
            jax.ShapeDtypeStruct((cells, 2, HALF), f32),
            jax.ShapeDtypeStruct((peers, 2 * kept, HALF), f32),
        ),
        in_specs=[SMEM] * 3 + [VMEM] * 6,
        out_specs=(VMEM,) * 4,
        scratch_shapes=tables
        + [pltpu.VMEM((2, P_SIZE, P_SIZE), f32), pltpu.VMEM((cells, P_SIZE, HALF), f32)],
        compiler_params=PARAMS,
    )(cell_counts, links, send, rec, rim_lo, rim_hi, recv, smoothing, energy)
    press_recv = exchange(press_out)
    press_lo, press_hi = neighbours(press_rec, "slab")

    state, leaving = pl.pallas_call(
        force_kernel,
        out_shape=(
            jax.ShapeDtypeStruct((6, cells, P_SIZE), f32),
            jax.ShapeDtypeStruct((6, peers * M), f32),
        ),
        in_specs=[SMEM] * 2 + [VMEM] * 13,
        out_specs=(VMEM, VMEM),
        scratch_shapes=tables
        + [
            pltpu.VMEM((width, 2, HALF), f32),
            pltpu.VMEM((width, V_ROWS, P_SIZE), jnp.bfloat16),
            pltpu.VMEM((2, P_SIZE, P_SIZE), f32),
            pltpu.VMEM((2, P_SIZE, P_SIZE), jnp.bfloat16),
            pltpu.VMEM((2, P_SIZE, P_SIZE), jnp.bfloat16),
            pltpu.VMEM((P_SIZE, HALF), f32),
        ],
        compiler_params=PARAMS,
    )(
        cell_counts, links, rec, rim_lo, rim_hi, recv, smoothing, press_rec, press_lo, press_hi, press_recv,
        positions, velocities, press, picks,
    )
    arrived = lax.all_to_all(leaving.reshape(6, peers, M), "sub", split_axis=1, concat_axis=1, tiled=True)
    return density, state, arrived.reshape(6, peers * M)


def solution(mesh):
    both = ("slab", "sub")
    return jax.shard_map(
        on_device,
        mesh=mesh,
        in_specs=(
            P(None, both, None),
            P(None, both, None),
            P(both, None),
            P(both, None),
            P(both, None),
            P(both),
            P(both, None, None),
            P(both, None),
            P(both, None, None),
            P(both, None),
        ),
        out_specs=(P(both, None), P(None, both, None), P(None, both)),
        check_vma=False,
    )
```

```python
import functools
import math

import jax
import jax.numpy as jnp
from jax import lax
from jax.experimental import pallas as pl
from jax.experimental.pallas import tpu as pltpu
from jax.sharding import PartitionSpec as P

P_SIZE = 256
HALF = 128
M = 8
NEAR = 2
K_ROWS = 32
V_ROWS = 32
STEP = 16
SIZES = tuple(range(128, P_SIZE + 1, STEP))
TINY = 1e-12
MASS_SCALE = 1024.0

adiabatic = 5.0 / 3.0
time_step = 0.05

f32 = jnp.float32
bf16 = jnp.bfloat16
VMEM = pl.BlockSpec(memory_space=pltpu.VMEM)
SMEM = pl.BlockSpec(memory_space=pltpu.SMEM)
LAST = (((1,), (1,)), ((), ()))
FIRST = (((0,), (0,)), ((), ()))


def dot(a, b, dims=(((1,), (0,)), ((), ()))):
    return lax.dot_general(a, b, dims, preferred_element_type=f32)


def shape(*dims):
    return jax.ShapeDtypeStruct(dims, f32)


def split(value):
    high = value.astype(bf16).astype(f32)
    rest = value - high
    mid = rest.astype(bf16).astype(f32)
    return high, mid, rest - mid


def row_ids():
    return lax.broadcasted_iota(jnp.int32, (8, HALF), 0)


def lanes():
    return lax.broadcasted_iota(jnp.int32, (1, P_SIZE), 1)


def swap(tile):
    return pltpu.roll(tile, 4, 0)


def is_fourth():
    return row_ids() % 4 == 3


def norms(tile):
    square = tile * tile
    return pltpu.roll(square, 1, 0) + pltpu.roll(square, 2, 0) + pltpu.roll(square, 3, 0)


def spread_fourth(tile):
    tile = jnp.where(is_fourth(), tile, 0.0)
    tile = tile + pltpu.roll(tile, 7, 0)
    return tile + pltpu.roll(tile, 6, 0)


def halves(first, second):
    top = row_ids() < 4
    return jnp.where(top, first, swap(second)), jnp.where(top, swap(first), second)


def by_row(parts):
    rows = row_ids()
    tile = 0.0
    for k, part in reversed(list(enumerate(parts))):
        tile = jnp.where(rows == k, part, tile)
    return tile


def right_operand(record, weighted):
    rows = row_ids()
    feature = jnp.where(is_fourth(), norms(record), record)
    if weighted:
        root = spread_fourth(record)
        feature = feature * (root * root)
    high, mid, low = split(feature)
    tiles = [halves(high, high), halves(mid, high), halves(low, mid)]
    if weighted:
        ones = []
        for value in halves(root * root, root * root):
            h, m, l = split(value)
            ones.append(jnp.where(rows < 3, h, jnp.where(rows < 5, m, jnp.where(rows < 6, l, 0.0))))
    else:
        ones = [jnp.where(rows < 3, 1.0, 0.0)] * 2
    parts = [jnp.concatenate([tile[k] for tile in tiles] + [ones[k]], axis=0) for k in range(2)]
    return jnp.concatenate(parts, axis=1).astype(bf16)


def left_operand(record, width):
    scale = 1.0 / (width * width)
    scale = jnp.where(row_ids() < 4, scale[:, :HALF], scale[:, HALF:])
    feature = scale * jnp.where(is_fourth(), 1.0, -2.0 * record)
    high, mid, low = split(feature)
    first, second = halves(high, mid), halves(high, low)
    own = spread_fourth(scale * norms(record))
    parts = []
    for k, value in enumerate(halves(own, own)):
        h, m, l = split(value)
        one = by_row([h, m, l, h, m, h])
        pad = jnp.zeros((HALF - K_ROWS, HALF), f32)
        parts.append(jnp.concatenate([first[k], second[k], first[k], one, pad], axis=0).T)
    return jnp.concatenate(parts, axis=0).astype(bf16)


def weight_operand(record, press):
    root = spread_fourth(record)
    plain = jnp.where(is_fourth(), 1.0, record) * (root * root * root * (1.0 / MASS_SCALE))
    pressed = plain * jnp.where(row_ids() < 4, press[0:1, :], press[1:2, :])
    tiles = [halves(*pair) for pair in zip(split(plain), split(pressed))]
    blank = jnp.zeros((8, HALF), f32)
    parts = [jnp.concatenate([tile[k] for tile in tiles] + [blank], axis=0) for k in range(2)]
    return jnp.concatenate(parts, axis=1).astype(bf16)


def sort_cells(counts, order, starts):
    cells = order.shape[0]
    kinds = [jnp.maximum(lax.div(counts[c] + (STEP - 1), STEP) - SIZES[0] // STEP, 0) for c in range(cells)]
    for c in range(cells):
        place = 0
        for other in range(cells):
            if other != c:
                ahead = kinds[other] <= kinds[c] if other < c else kinds[other] < kinds[c]
                place = place + ahead.astype(jnp.int32)
        order[place] = jnp.int32(c)
    for k in range(starts.shape[0]):
        starts[k] = sum((kind < k).astype(jnp.int32) for kind in kinds)


def pack_kernel(counts, send, pos, mass, rec, first, last, out, order, starts):
    cells = mass.shape[0]
    sort_cells(counts, order, starts)
    scaled = mass[...] * MASS_SCALE
    root = jnp.exp(jnp.log(scaled) * (1.0 / 3.0))
    for _ in range(2):
        root = root - (root * root * root - scaled) / (3.0 * root * root)
    for c in range(cells):
        live = lanes() < counts[c]
        for k in range(4):
            row = pos[k, c : c + 1, :] - 0.5 if k < 3 else root[c : c + 1, :]
            row = jnp.where(live, row, 0.0)
            rec[c, k : k + 1, :] = row[:, :HALF]
            rec[c, k + 4 : k + 5, :] = row[:, HALF:]
    first[0] = rec[0]
    last[0] = rec[cells - 1]
    for v in range(out.shape[0]):
        for k in range(send.shape[0]):
            out[v, 8 * k : 8 * k + 8, :] = rec[send[k, v]]


def fill_table(table, rec, rim_lo, rim_hi, recv, rows):
    cells = rec.shape[0]
    table[0] = rim_lo[0]
    for c in range(cells):
        table[1 + c] = rec[c]
    table[cells + 1] = rim_hi[0]
    if recv is not None:
        per_peer = recv.shape[1] // rows
        for v in range(recv.shape[0]):
            for k in range(per_peer):
                table[cells + 2 + v * per_peer + k] = recv[v, rows * k : rows * k + rows, :]


def for_cells(count, step):
    unroll = 4
    done = count - count % unroll

    def body(t, carry):
        step(t)
        return carry

    lax.fori_loop(0, done, body, 0, unroll=unroll)
    for t in range(done, count):
        step(t)


def fill_left(rec, smoothing, left):
    for c in range(rec.shape[0]):
        left[c] = left_operand(rec[c], smoothing[c : c + 1, :])


def by_size(order, starts, run):
    cells = order.shape[0]
    for k, size in enumerate(SIZES):

        def step(n, carry, size=size):
            run(order[n], order[jnp.maximum(n - 1, 0)], order[jnp.minimum(n + 1, cells - 1)], size)
            return carry

        lax.fori_loop(starts[k], starts[k + 1], step, 0)


def density_sums(
    order, starts, partners, groups, table, right, left, square, total, inner_total, value_high, value_low, store
):
    slots = len(groups)

    def product(c, g, size):
        for k, p in enumerate(groups[g]):
            square[k, :size, :] = dot(left[c, :size, :K_ROWS], right[partners[p, c]])

    def reduce():
        ones = jnp.ones((8, HALF), bf16)
        return (dot(ones, value_high[...], LAST) + dot(ones, value_low[...], LAST))[0:1, :]

    def run(c, before, after, size):
        for g, group in enumerate(groups):
            if g == 0:
                store(before, reduce())
            roots = [table[partners[p, c], r : r + 1, :] for p in group for r in (3, 7)]
            doubled = [root + root for root in roots]
            for base in range(0, size, STEP):
                block = pl.ds(base, STEP)
                outer_sum = inner_sum = None
                for k in range(len(roots)):
                    half = slice((k % 2) * HALF, (k % 2 + 1) * HALF)
                    s = jnp.maximum(square[k // 2, block, half], TINY)
                    outer = jnp.maximum(doubled[k] - s * lax.rsqrt(s), 0.0)
                    inner = jnp.maximum(outer - roots[k], 0.0)
                    outer = outer * outer * outer
                    inner = inner * inner * inner
                    outer_sum = outer if k == 0 else outer_sum + outer
                    inner_sum = inner if k == 0 else inner_sum + inner
                if g:
                    outer_sum = total[block, :] + outer_sum
                    inner_sum = inner_total[block, :] + inner_sum
                if g + 1 < slots:
                    total[block, :] = outer_sum
                    inner_total[block, :] = inner_sum
                else:
                    value = 0.25 * outer_sum - inner_sum
                    high = value.astype(bf16)
                    value_high[block, :] = high
                    value_low[block, :] = (value - high.astype(f32)).astype(bf16)
            if g + 1 < slots:
                product(c, g + 1, size)
            else:
                product(after, 0, P_SIZE)

    product(order[0], 0, P_SIZE)
    by_size(order, starts, run)
    store(order[order.shape[0] - 1], reduce())


def near_density_kernel(
    order, starts, partners, rec, rim_lo, rim_hi, smoothing, sums, left, table, right, *scratch
):
    fill_table(table, rec, rim_lo, rim_hi, None, 8)
    fill_left(rec, smoothing, left)

    def step(t):
        right[t] = right_operand(table[t], True)

    for_cells(table.shape[0], step)

    def store(c, row):
        sums[pl.ds(c, 1), :] = row

    density_sums(order, starts, partners, [(0,), (1,)], table, right, left, *scratch, store)


def density_kernel(
    order, starts, partners, counts, send, rec, rim_lo, rim_hi, recv, left, smoothing, energy, near,
    density, press, press_rec, first, last, press_send,
    table, right, sums, *scratch,
):
    cells = rec.shape[0]
    fill_table(table, rec, rim_lo, rim_hi, recv, 8)

    def step(t):
        right[t] = right_operand(table[t], True)

    for_cells(table.shape[0], step)

    def store(c, row):
        sums[pl.ds(c, 1), :] = row

    pairs = partners.shape[0]
    groups = [tuple(range(p, min(p + 2, pairs))) for p in range(NEAR, pairs, 2)]
    density_sums(order, starts, partners, groups, table, right, left, *scratch, store)
    for c in range(cells):
        width = smoothing[c : c + 1, :]
        live = lanes() < counts[c]
        mass = (near[c : c + 1, :] + sums[c : c + 1, :]) * (1.0 / MASS_SCALE)
        rho = mass / (math.pi * width * width * width)
        density[c : c + 1, :] = jnp.where(live, rho, 0.0)
        value = jnp.where(
            live, (adiabatic - 1.0) * energy[c : c + 1, :] / jnp.where(live, rho, 1.0), 0.0
        )
        press[c : c + 1, :] = value
        press_rec[c, 0:1, :] = value[:, :HALF]
        press_rec[c, 1:2, :] = value[:, HALF:]
    first[0] = press_rec[0]
    last[0] = press_rec[cells - 1]
    for v in range(send.shape[1]):
        for k in range(send.shape[0]):
            press_send[v, 2 * k : 2 * k + 2, :] = press_rec[send[k, v]]


def force_sums(
    order, starts, partners, columns, right, left, weights, square, slope_high, slope_low, total, store
):
    count = len(columns)

    def product(c, n, size):
        square[n % 2, :size, :] = dot(left[c, :size, :K_ROWS], right[partners[columns[n], c]])

    def gather(c, n, size):
        w = weights[partners[columns[n], c]]
        return dot(w, slope_high[n % 2, :size, :], LAST) + dot(w, slope_low[n % 2, :size, :], LAST)

    def finish(c):
        found = total[...] + gather(c, count - 1, P_SIZE)
        store(c, found[0:8, :] + found[8:16, :] + found[16:24, :])

    def run(c, before, after, size):
        added = None
        for n in range(count):
            if n + 1 < count:
                product(c, n + 1, size)
            else:
                product(after, 0, P_SIZE)
            if n == 0:
                finish(before)
            else:
                more = gather(c, n - 1, size)
                added = more if n == 1 else added + more
            for base in range(0, size, STEP):
                block = pl.ds(base, STEP)
                s = jnp.minimum(jnp.maximum(square[n % 2, block, :], TINY), 4.0)
                y = lax.rsqrt(s)
                q = s * y
                f = (jnp.minimum(y, 1.0) - 1.0) + (jnp.maximum(q, 1.0) - 0.75 * q)
                high = f.astype(bf16)
                slope_high[n % 2, block, :] = high
                slope_low[n % 2, block, :] = (f - high.astype(f32)).astype(bf16)
        total[:, :size] = added

    product(order[0], 0, P_SIZE)
    by_size(order, starts, run)
    finish(order[order.shape[0] - 1])


def near_force_kernel(
    order, starts, partners, rec, rim_lo, rim_hi, left, press_rec, press_lo, press_hi, sums,
    table, right, press_table, weights, square, slope_high, slope_low, total,
):
    fill_table(table, rec, rim_lo, rim_hi, None, 8)
    fill_table(press_table, press_rec, press_lo, press_hi, None, 2)

    def step(t):
        right[t] = right_operand(table[t], False)
        weights[t] = weight_operand(table[t], press_table[t])

    for_cells(table.shape[0], step)

    def store(c, found):
        sums[c] = found

    force_sums(
        order, starts, partners, list(range(NEAR)), right, left, weights, square, slope_high, slope_low, total, store
    )


def slot_maps(slots, peers):
    block = lax.broadcasted_iota(jnp.int32, (peers, slots), 1) // M
    owner = (block == lax.broadcasted_iota(jnp.int32, (peers, slots), 0)).astype(f32).astype(bf16)
    column = lax.broadcasted_iota(jnp.int32, (slots, HALF), 1)
    slot = lax.broadcasted_iota(jnp.int32, (slots, HALF), 0)
    return owner, column % M == slot % M


def field_map():
    field = lax.broadcasted_iota(jnp.int32, (8, HALF), 1) // M
    return (field == lax.broadcasted_iota(jnp.int32, (8, HALF), 0)).astype(f32)


def force_kernel(
    order, starts, partners, counts, rec, rim_lo, rim_hi, recv, left, press_rec, press_lo, press_hi, press_recv,
    smoothing, pos, vel, press, near, picks,
    state, leaving,
    table, right, press_table, weights, square, slope_high, slope_low, total,
):
    cells = rec.shape[0]
    fill_table(table, rec, rim_lo, rim_hi, recv, 8)
    fill_table(press_table, press_rec, press_lo, press_hi, press_recv, 2)

    def step(t):
        right[t] = right_operand(table[t], False)
        weights[t] = weight_operand(table[t], press_table[t])

    for_cells(table.shape[0], step)

    def store(c, found):
        sums = near[c] + found
        width = smoothing[pl.ds(c, 1), :]
        squared = width * width
        factor = (3.0 * time_step / math.pi) / (squared * squared * width)
        own = press[pl.ds(c, 1), :]
        live = lanes() < counts[c]
        for k in range(3):
            place = pos[k, pl.ds(c, 1), :]
            centred = place - 0.5
            push = own * (centred * sums[3:4, :] - sums[k : k + 1, :]) + (
                centred * sums[7:8, :] - sums[4 + k : 5 + k, :]
            )
            speed = vel[k, pl.ds(c, 1), :] + factor * push
            state[k, pl.ds(c, 1), :] = jnp.where(live, place + time_step * speed, 0.0)
            state[3 + k, pl.ds(c, 1), :] = jnp.where(live, speed, 0.0)

    force_sums(
        order, starts, partners, list(range(NEAR, partners.shape[0])), right, left, weights, square,
        slope_high, slope_low, total, store,
    )

    slots = picks.shape[1]
    picked = picks[...]
    chosen = lax.broadcasted_iota(jnp.int32, (P_SIZE, slots), 0) == picked % P_SIZE
    chosen = chosen.astype(f32).astype(bf16)
    mine = lax.broadcasted_iota(jnp.int32, (cells, slots), 0) == picked // P_SIZE
    parts = [split(state[k]) for k in range(6)]
    parts = jnp.concatenate([part[n] for n in range(3) for part in parts], axis=0).astype(bf16)
    found = dot(parts, chosen)
    rows = []
    for k in range(6):
        value = sum(found[(6 * n + k) * cells : (6 * n + k + 1) * cells, :] for n in range(3))
        rows.append(jnp.sum(jnp.where(mine, value, 0.0), axis=0, keepdims=True))
    found = jnp.concatenate(rows + [jnp.zeros((2, slots), f32)], axis=0)
    owner, same = slot_maps(slots, leaving.shape[0])
    spread = field_map()
    blank = jnp.zeros_like(spread)
    spread = jnp.concatenate(
        [jnp.concatenate([spread if n == k else blank for n in range(3)], axis=1) for k in range(3)], axis=0
    )
    wide = dot(jnp.concatenate(split(found), axis=0).astype(bf16), spread.astype(bf16), FIRST)
    wide = jnp.concatenate(
        [jnp.where(same, wide[:, HALF * n : HALF * (n + 1)], 0.0) for n in range(3)], axis=1
    )
    value = dot(owner, wide.astype(bf16))
    leaving[...] = sum(value[:, HALF * n : HALF * (n + 1)] for n in range(3))


def arrive_kernel(arrived, out):
    owner, same = slot_maps(out.shape[1], arrived.shape[0])
    wide = dot(owner, jnp.concatenate(split(arrived[...]), axis=1).astype(bf16), FIRST)
    wide = jnp.concatenate(
        [jnp.where(same, wide[:, HALF * n : HALF * (n + 1)], 0.0) for n in range(3)], axis=1
    )
    spread = field_map()
    value = dot(jnp.concatenate([spread] * 3, axis=1).astype(bf16), wide.astype(bf16), LAST)
    out[...] = value[: out.shape[0], :]


def call(kernel, outs, smem, vmem, scratch=(), limit=48):
    return pl.pallas_call(
        kernel,
        out_shape=tuple(outs),
        in_specs=[SMEM] * len(smem) + [VMEM] * len(vmem),
        out_specs=tuple(SMEM if out.dtype == jnp.int32 else VMEM for out in outs),
        scratch_shapes=scratch,
        compiler_params=pltpu.CompilerParams(vmem_limit_bytes=limit * 1024 * 1024),
    )(*smem, *vmem)


def to_neighbours(first, last, axis):
    count = lax.axis_size(axis)
    up = [(i, (i + 1) % count) for i in range(count)]
    down = [(j, i) for i, j in up]
    return lax.ppermute(last, axis, up), lax.ppermute(first, axis, down)


def exchange(value):
    return lax.all_to_all(value, "sub", split_axis=0, concat_axis=0, tiled=True)


def on_device(
    positions, velocities, mass, smoothing, energy, cell_counts, send_cells, partners, mig_list, mig_counts
):
    cells = mass.shape[0]
    peers = lax.axis_size("sub")
    kept = send_cells.shape[2]
    near_width = cells + 2
    full_width = near_width + peers * kept
    send = send_cells[0].T
    links = partners.T

    rec, first, last, outgoing, order, starts = call(
        pack_kernel,
        [
            shape(cells, 8, HALF),
            shape(1, 8, HALF),
            shape(1, 8, HALF),
            shape(peers, 8 * kept, HALF),
            jax.ShapeDtypeStruct((cells,), jnp.int32),
            jax.ShapeDtypeStruct((len(SIZES) + 1,), jnp.int32),
        ],
        [cell_counts, send],
        [positions, mass],
        limit=60,
    )
    recv = exchange(outgoing)
    rim_lo, rim_hi = to_neighbours(first, last, "slab")

    keep = jnp.arange(M)[None, :] < mig_counts[0][:, None]
    picks = jnp.where(keep, mig_list[0], -P_SIZE).reshape(1, peers * M)

    def tables(width):
        return [
            pltpu.VMEM((width, 8, HALF), f32),
            pltpu.VMEM((width, K_ROWS, P_SIZE), bf16),
        ]

    def sums(size):
        return [
            pltpu.VMEM((size, P_SIZE, P_SIZE), f32),
            pltpu.VMEM((P_SIZE, HALF), f32),
            pltpu.VMEM((P_SIZE, HALF), f32),
            pltpu.VMEM((P_SIZE, HALF), bf16),
            pltpu.VMEM((P_SIZE, HALF), bf16),
        ]

    near, left = call(
        near_density_kernel,
        [shape(cells, P_SIZE), jax.ShapeDtypeStruct((cells, P_SIZE, HALF), bf16)],
        [order, starts, links],
        [rec, rim_lo, rim_hi, smoothing],
        tables(near_width) + sums(1),
    )
    density, press, press_rec, first, last, press_out = call(
        density_kernel,
        [
            shape(cells, P_SIZE),
            shape(cells, P_SIZE),
            shape(cells, 2, HALF),
            shape(1, 2, HALF),
            shape(1, 2, HALF),
            shape(peers, 2 * kept, HALF),
        ],
        [order, starts, links, cell_counts, send],
        [rec, rim_lo, rim_hi, recv, left, smoothing, energy, near],
        tables(full_width) + [pltpu.VMEM((cells, P_SIZE), f32)] + sums(2),
    )
    press_recv = exchange(press_out)
    press_lo, press_hi = to_neighbours(first, last, "slab")

    def force_tables(width):
        return tables(width) + [
            pltpu.VMEM((width, 2, HALF), f32),
            pltpu.VMEM((width, V_ROWS, P_SIZE), bf16),
            pltpu.VMEM((2, P_SIZE, P_SIZE), f32),
            pltpu.VMEM((2, P_SIZE, P_SIZE), bf16),
            pltpu.VMEM((2, P_SIZE, P_SIZE), bf16),
            pltpu.VMEM((V_ROWS, P_SIZE), f32),
        ]

    (near,) = call(
        near_force_kernel,
        [shape(cells, 8, P_SIZE)],
        [order, starts, links],
        [rec, rim_lo, rim_hi, left, press_rec, press_lo, press_hi],
        force_tables(near_width),
    )
    state, leaving = call(
        force_kernel,
        [shape(6, cells, P_SIZE), shape(peers, HALF)],
        [order, starts, links, cell_counts],
        [
            rec, rim_lo, rim_hi, recv, left, press_rec, press_lo, press_hi, press_recv,
            smoothing, positions, velocities, press, near, picks,
        ],
        force_tables(full_width),
    )
    arrived = exchange(leaving.reshape(peers, 1, HALF)).reshape(peers, HALF)
    (arrivals,) = call(arrive_kernel, [shape(6, peers * M)], [], [arrived])
    return density, state, arrivals


def solution(mesh):
    both = ("slab", "sub")
    return jax.shard_map(
        on_device,
        mesh=mesh,
        in_specs=(
            P(None, both, None),
            P(None, both, None),
            P(both, None),
            P(both, None),
            P(both, None),
            P(both),
            P(both, None, None),
            P(both, None),
            P(both, None, None),
            P(both, None),
        ),
        out_specs=(P(both, None), P(None, both, None), P(None, both)),
        check_vma=False,
    )
```

```python
import functools
import math

import jax
import jax.numpy as jnp
from jax import lax
from jax.experimental import pallas as pl
from jax.experimental.pallas import tpu as pltpu
from jax.sharding import PartitionSpec as P

P_SIZE = 256
HALF = 128
M = 8
NEAR = 2
K_ROWS = 32
V_ROWS = 32
STEP = 16
SIZES = tuple(range(128, P_SIZE + 1, STEP))
TINY = 1e-12
MASS_SCALE = 1024.0

adiabatic = 5.0 / 3.0
time_step = 0.05

f32 = jnp.float32
bf16 = jnp.bfloat16
VMEM = pl.BlockSpec(memory_space=pltpu.VMEM)
SMEM = pl.BlockSpec(memory_space=pltpu.SMEM)
HBM = pl.BlockSpec(memory_space=pl.ANY)
LAST = (((1,), (1,)), ((), ()))
FIRST = (((0,), (0,)), ((), ()))


def dot(a, b, dims=(((1,), (0,)), ((), ()))):
    return lax.dot_general(a, b, dims, preferred_element_type=f32)


def shape(*dims):
    return jax.ShapeDtypeStruct(dims, f32)


def split(value):
    high = value.astype(bf16).astype(f32)
    rest = value - high
    mid = rest.astype(bf16).astype(f32)
    return high, mid, rest - mid


def row_ids():
    return lax.broadcasted_iota(jnp.int32, (8, HALF), 0)


def lanes():
    return lax.broadcasted_iota(jnp.int32, (1, P_SIZE), 1)


def live_slots(rec):
    rows = [
        jnp.concatenate([rec[c, 3:4, :], rec[c, 7:8, :]], axis=1) for c in range(rec.shape[0])
    ]
    return jnp.concatenate(rows, axis=0) > 0.0


def swap(tile):
    return pltpu.roll(tile, 4, 0)


def is_fourth():
    return row_ids() % 4 == 3


def norms(tile):
    square = tile * tile
    return pltpu.roll(square, 1, 0) + pltpu.roll(square, 2, 0) + pltpu.roll(square, 3, 0)


def spread_fourth(tile):
    tile = jnp.where(is_fourth(), tile, 0.0)
    tile = tile + pltpu.roll(tile, 7, 0)
    return tile + pltpu.roll(tile, 6, 0)


def halves(first, second):
    top = row_ids() < 4
    return jnp.where(top, first, swap(second)), jnp.where(top, swap(first), second)


def by_row(parts):
    rows = row_ids()
    tile = 0.0
    for k, part in reversed(list(enumerate(parts))):
        tile = jnp.where(rows == k, part, tile)
    return tile


def right_operand(record, weighted):
    rows = row_ids()
    feature = jnp.where(is_fourth(), norms(record), record)
    if weighted:
        root = spread_fourth(record)
        feature = feature * (root * root)
    high, mid, low = split(feature)
    tiles = [halves(high, high), halves(mid, high), halves(low, mid)]
    if weighted:
        ones = []
        for value in halves(root * root, root * root):
            h, m, l = split(value)
            ones.append(jnp.where(rows < 3, h, jnp.where(rows < 5, m, jnp.where(rows < 6, l, 0.0))))
    else:
        ones = [jnp.where(rows < 3, 1.0, 0.0)] * 2
    parts = [jnp.concatenate([tile[k] for tile in tiles] + [ones[k]], axis=0) for k in range(2)]
    return jnp.concatenate(parts, axis=1).astype(bf16)


def left_operand(record, width):
    scale = 1.0 / (width * width)
    scale = jnp.where(row_ids() < 4, scale[:, :HALF], scale[:, HALF:])
    feature = scale * jnp.where(is_fourth(), 1.0, -2.0 * record)
    high, mid, low = split(feature)
    first, second = halves(high, mid), halves(high, low)
    own = spread_fourth(scale * norms(record))
    parts = []
    for k, value in enumerate(halves(own, own)):
        h, m, l = split(value)
        one = by_row([h, m, l, h, m, h])
        pad = jnp.zeros((HALF - K_ROWS, HALF), f32)
        parts.append(jnp.concatenate([first[k], second[k], first[k], one, pad], axis=0).T)
    return jnp.concatenate(parts, axis=0).astype(bf16)


def weight_operand(record, press):
    root = spread_fourth(record)
    plain = jnp.where(is_fourth(), 1.0, record) * (root * root * root * (1.0 / MASS_SCALE))
    pressed = plain * jnp.where(row_ids() < 4, press[0:1, :], press[1:2, :])
    tiles = [halves(*pair) for pair in zip(split(plain), split(pressed))]
    blank = jnp.zeros((8, HALF), f32)
    parts = [jnp.concatenate([tile[k] for tile in tiles] + [blank], axis=0) for k in range(2)]
    return jnp.concatenate(parts, axis=1).astype(bf16)


def sort_cells(counts, order):
    cells = order.shape[0]
    keys = []
    for c in range(cells):
        kind = jnp.maximum(lax.div(counts[c] + (STEP - 1), STEP) - SIZES[0] // STEP, 0)
        keys.append(kind * cells + c)
    places = [cells - 1 - c for c in range(cells)]
    for c in range(cells):
        for other in range(c + 1, cells):
            behind = (keys[c] > keys[other]).astype(jnp.int32)
            places[c] = places[c] + (behind - 1)
            places[other] = places[other] + (1 - behind)
    for c in range(cells):
        order[places[c]] = keys[c]


def pack_kernel(counts, send, pos, mass, rec, first, last, out):
    cells = mass.shape[0]
    scaled = mass[...] * MASS_SCALE
    root = jnp.exp(jnp.log(scaled) * (1.0 / 3.0))
    for _ in range(2):
        root = root - (root * root * root - scaled) / (3.0 * root * root)
    for c in range(cells):
        live = lanes() < counts[c]
        for k in range(4):
            row = pos[k, c : c + 1, :] - 0.5 if k < 3 else root[c : c + 1, :]
            row = jnp.where(live, row, 0.0)
            rec[c, k : k + 1, :] = row[:, :HALF]
            rec[c, k + 4 : k + 5, :] = row[:, HALF:]
    first[0] = rec[0]
    last[0] = rec[cells - 1]
    for v in range(out.shape[0]):
        for k in range(send.shape[0]):
            out[v, 8 * k : 8 * k + 8, :] = rec[send[k, v]]


def fill_table(table, rec, rim_lo, rim_hi, recv, rows):
    cells = rec.shape[0]
    table[0] = rim_lo[0]
    for c in range(cells):
        table[1 + c] = rec[c]
    table[cells + 1] = rim_hi[0]
    if recv is not None:
        per_peer = recv.shape[1] // rows
        for v in range(recv.shape[0]):
            for k in range(per_peer):
                table[cells + 2 + v * per_peer + k] = recv[v, rows * k : rows * k + rows, :]


def for_cells(count, step):
    unroll = 4
    done = count - count % unroll

    def body(t, carry):
        step(t)
        return carry

    lax.fori_loop(0, done, body, 0, unroll=unroll)
    for t in range(done, count):
        step(t)


def fill_left(rec, smoothing, left):
    for c in range(rec.shape[0]):
        left[c] = left_operand(rec[c], smoothing[c : c + 1, :])


def cell_at(order, n):
    cells = order.shape[0]
    return lax.rem(order[jnp.clip(n, 0, cells - 1)], cells)


def by_size(order, run):
    cells = order.shape[0]
    done = jnp.int32(0)
    for k, size in enumerate(SIZES):

        def more(n, k=k):
            return (n < cells) & (order[jnp.minimum(n, cells - 1)] < (k + 1) * cells)

        def step(n, size=size):
            run(cell_at(order, n), cell_at(order, n - 1), cell_at(order, n + 1), size)
            return n + 1

        done = lax.while_loop(more, step, done)


def density_sums(
    order, partners, groups, table, right, left, square, total, inner_total, value_high, value_low, store
):
    slots = len(groups)

    def product(c, g, size):
        for k, p in enumerate(groups[g]):
            square[k, :size, :] = jnp.maximum(dot(left[c, :size, :K_ROWS], right[partners[p, c]]), TINY)

    def reduce():
        ones = jnp.ones((8, HALF), bf16)
        return (dot(ones, value_high[...], LAST) + dot(ones, value_low[...], LAST))[0:1, :]

    def run(c, before, after, size):
        for g, group in enumerate(groups):
            if g == 0:
                store(before, reduce())
            roots = [table[partners[p, c], r : r + 1, :] for p in group for r in (3, 7)]
            doubled = [root + root for root in roots]
            for base in range(0, size, STEP):
                block = pl.ds(base, STEP)
                outer_sum = inner_sum = None
                for k in range(len(roots)):
                    half = slice((k % 2) * HALF, (k % 2 + 1) * HALF)
                    s = square[k // 2, block, half]
                    outer = jnp.maximum(doubled[k] - s * lax.rsqrt(s), 0.0)
                    inner = jnp.maximum(outer - roots[k], 0.0)
                    outer = outer * outer * outer
                    inner = inner * inner * inner
                    outer_sum = outer if k == 0 else outer_sum + outer
                    inner_sum = inner if k == 0 else inner_sum + inner
                if g:
                    outer_sum = total[block, :] + outer_sum
                    inner_sum = inner_total[block, :] + inner_sum
                if g + 1 < slots:
                    total[block, :] = outer_sum
                    inner_total[block, :] = inner_sum
                else:
                    value = 0.25 * outer_sum - inner_sum
                    high = value.astype(bf16)
                    value_high[block, :] = high
                    value_low[block, :] = (value - high.astype(f32)).astype(bf16)
            if g + 1 < slots:
                product(c, g + 1, size)
            else:
                product(after, 0, P_SIZE)

    product(cell_at(order, 0), 0, P_SIZE)
    by_size(order, run)
    store(cell_at(order, order.shape[0] - 1), reduce())


class near_partners:
    def __init__(self, cells):
        self.cells = cells

    def __getitem__(self, place):
        p, c = place
        return c + 1 if p == 0 else jnp.where(c < self.cells // 2, 0, self.cells + 1)


def near_density_kernel(
    counts_ref, rec, rim_lo, rim_hi, smoothing, sums, left, order, table, right, counts, copied, *scratch
):
    copy = pltpu.make_async_copy(counts_ref, counts, copied)
    copy.start()
    fill_table(table, rec, rim_lo, rim_hi, None, 8)
    fill_left(rec, smoothing, left)

    def step(t):
        right[t] = right_operand(table[t], True)

    for_cells(table.shape[0], step)
    copy.wait()
    sort_cells(counts, order)

    def store(c, row):
        sums[pl.ds(c, 1), :] = row

    density_sums(order, near_partners(rec.shape[0]), [(0,), (1,)], table, right, left, *scratch, store)


def density_kernel(
    order, partners, send_ref, rec, rim_lo, rim_hi, recv, left, smoothing, energy, near,
    density, press, press_rec, first, last, press_send,
    table, right, sums, send, copied, *scratch,
):
    cells = rec.shape[0]
    copy = pltpu.make_async_copy(send_ref, send, copied)
    copy.start()
    fill_table(table, rec, rim_lo, rim_hi, recv, 8)

    def step(t):
        right[t] = right_operand(table[t], True)

    for_cells(table.shape[0], step)

    def store(c, row):
        sums[pl.ds(c, 1), :] = row

    pairs = partners.shape[0]
    groups = [tuple(range(p, min(p + 2, pairs))) for p in range(NEAR, pairs, 2)]
    density_sums(order, partners, groups, table, right, left, *scratch, store)
    width = smoothing[...]
    live = live_slots(rec)
    rho = (near[...] + sums[...]) * (1.0 / MASS_SCALE) / (math.pi * width * width * width)
    density[...] = jnp.where(live, rho, 0.0)
    value = jnp.where(live, (adiabatic - 1.0) * energy[...] / jnp.where(live, rho, 1.0), 0.0)
    press[...] = value
    for c in range(cells):
        press_rec[c, 0:1, :] = value[c : c + 1, :HALF]
        press_rec[c, 1:2, :] = value[c : c + 1, HALF:]
    first[0] = press_rec[0]
    last[0] = press_rec[cells - 1]
    copy.wait()
    for v in range(send.shape[1]):
        for k in range(send.shape[0]):
            press_send[v, 2 * k : 2 * k + 2, :] = press_rec[send[k, v]]


def force_sums(
    order, partners, columns, right, left, weights, square, slope_high, slope_low, total, store
):
    count = len(columns)
    slots = square.shape[0]
    ahead = slots - 1

    def product(c, n, size):
        square[n % slots, :size, :] = jnp.minimum(jnp.maximum(dot(left[c, :size, :K_ROWS], right[partners[columns[n], c]]), TINY), 4.0)

    def gather(c, n, size):
        w = weights[partners[columns[n], c]]
        return dot(w, slope_high[n % 2, :size, :], LAST) + dot(w, slope_low[n % 2, :size, :], LAST)

    def finish(c):
        found = total[...] + gather(c, count - 1, P_SIZE)
        store(c, found[0:8, :] + found[8:16, :] + found[16:24, :])

    def run(c, before, after, size):
        added = None
        for n in range(count):
            if n + ahead < count:
                product(c, n + ahead, size)
            else:
                product(after, n + ahead - count, P_SIZE)
            if n == 0:
                finish(before)
            else:
                more = gather(c, n - 1, size)
                added = more if n == 1 else added + more
            for base in range(0, size, STEP):
                block = pl.ds(base, STEP)
                s = square[n % slots, block, :]
                y = lax.rsqrt(s)
                q = s * y
                f = (jnp.minimum(y, 1.0) - 1.0) + (jnp.maximum(q, 1.0) - 0.75 * q)
                high = f.astype(bf16)
                slope_high[n % 2, block, :] = high
                slope_low[n % 2, block, :] = (f - high.astype(f32)).astype(bf16)
        total[:, :size] = added

    for n in range(ahead):
        product(cell_at(order, 0), n, P_SIZE)
    by_size(order, run)
    finish(cell_at(order, order.shape[0] - 1))


def near_force_kernel(
    order, rec, rim_lo, rim_hi, left, press_rec, press_lo, press_hi, sums,
    table, right, press_table, weights, square, slope_high, slope_low, total,
):
    fill_table(table, rec, rim_lo, rim_hi, None, 8)
    fill_table(press_table, press_rec, press_lo, press_hi, None, 2)

    def step(t):
        right[t] = right_operand(table[t], False)
        weights[t] = weight_operand(table[t], press_table[t])

    for_cells(table.shape[0], step)

    def store(c, found):
        sums[c] = found

    force_sums(
        order, near_partners(rec.shape[0]), list(range(NEAR)), right, left, weights, square, slope_high, slope_low, total, store
    )


def slot_maps(slots, peers):
    block = lax.broadcasted_iota(jnp.int32, (peers, slots), 1) // M
    owner = (block == lax.broadcasted_iota(jnp.int32, (peers, slots), 0)).astype(f32).astype(bf16)
    column = lax.broadcasted_iota(jnp.int32, (slots, HALF), 1)
    slot = lax.broadcasted_iota(jnp.int32, (slots, HALF), 0)
    return owner, column % M == slot % M


def field_map():
    field = lax.broadcasted_iota(jnp.int32, (8, HALF), 1) // M
    return (field == lax.broadcasted_iota(jnp.int32, (8, HALF), 0)).astype(f32)


def force_kernel(
    order, partners, rec, rim_lo, rim_hi, recv, left, press_rec, press_lo, press_hi, press_recv,
    smoothing, pos, vel, press, near, picks,
    state, leaving,
    table, right, press_table, weights, square, slope_high, slope_low, total, sums,
):
    cells = rec.shape[0]
    fill_table(table, rec, rim_lo, rim_hi, recv, 8)
    fill_table(press_table, press_rec, press_lo, press_hi, press_recv, 2)

    def step(t):
        right[t] = right_operand(table[t], False)
        weights[t] = weight_operand(table[t], press_table[t])

    for_cells(table.shape[0], step)

    def store(c, found):
        found = near[c] + found
        for k in range(8):
            sums[k, pl.ds(c, 1), :] = found[k : k + 1, :]

    force_sums(
        order, partners, list(range(NEAR, partners.shape[0])), right, left, weights, square,
        slope_high, slope_low, total, store,
    )

    width = smoothing[...]
    squared = width * width
    factor = (3.0 * time_step / math.pi) / (squared * squared * width)
    own = press[...]
    live = live_slots(rec)
    for k in range(3):
        place = pos[k]
        centred = place - 0.5
        push = own * (centred * sums[3] - sums[k]) + (centred * sums[7] - sums[4 + k])
        speed = vel[k] + factor * push
        state[k] = jnp.where(live, place + time_step * speed, 0.0)
        state[3 + k] = jnp.where(live, speed, 0.0)

    slots = picks.shape[1]
    picked = picks[...]
    chosen = lax.broadcasted_iota(jnp.int32, (P_SIZE, slots), 0) == picked % P_SIZE
    chosen = chosen.astype(f32).astype(bf16)
    mine = lax.broadcasted_iota(jnp.int32, (cells, slots), 0) == picked // P_SIZE
    parts = [split(state[k]) for k in range(6)]
    parts = jnp.concatenate([part[n] for n in range(3) for part in parts], axis=0).astype(bf16)
    found = dot(parts, chosen)
    rows = []
    for k in range(6):
        value = sum(found[(6 * n + k) * cells : (6 * n + k + 1) * cells, :] for n in range(3))
        rows.append(jnp.sum(jnp.where(mine, value, 0.0), axis=0, keepdims=True))
    found = jnp.concatenate(rows + [jnp.zeros((2, slots), f32)], axis=0)
    owner, same = slot_maps(slots, leaving.shape[0])
    spread = field_map()
    blank = jnp.zeros_like(spread)
    spread = jnp.concatenate(
        [jnp.concatenate([spread if n == k else blank for n in range(3)], axis=1) for k in range(3)], axis=0
    )
    wide = dot(jnp.concatenate(split(found), axis=0).astype(bf16), spread.astype(bf16), FIRST)
    wide = jnp.concatenate(
        [jnp.where(same, wide[:, HALF * n : HALF * (n + 1)], 0.0) for n in range(3)], axis=1
    )
    value = dot(owner, wide.astype(bf16))
    leaving[...] = sum(value[:, HALF * n : HALF * (n + 1)] for n in range(3))


def arrive_kernel(arrived, out):
    owner, same = slot_maps(out.shape[1], arrived.shape[0])
    wide = dot(owner, jnp.concatenate(split(arrived[...]), axis=1).astype(bf16), FIRST)
    wide = jnp.concatenate(
        [jnp.where(same, wide[:, HALF * n : HALF * (n + 1)], 0.0) for n in range(3)], axis=1
    )
    spread = field_map()
    value = dot(jnp.concatenate([spread] * 3, axis=1).astype(bf16), wide.astype(bf16), LAST)
    out[...] = value[: out.shape[0], :]


def call(kernel, outs, smem, hbm, vmem, scratch=(), limit=48):
    return pl.pallas_call(
        kernel,
        out_shape=tuple(outs),
        in_specs=[SMEM] * len(smem) + [HBM] * len(hbm) + [VMEM] * len(vmem),
        out_specs=tuple(SMEM if out.dtype == jnp.int32 else VMEM for out in outs),
        scratch_shapes=scratch,
        compiler_params=pltpu.CompilerParams(vmem_limit_bytes=limit * 1024 * 1024),
    )(*smem, *hbm, *vmem)


def to_neighbours(first, last, axis):
    count = lax.axis_size(axis)
    up = [(i, (i + 1) % count) for i in range(count)]
    down = [(j, i) for i, j in up]
    return lax.ppermute(last, axis, up), lax.ppermute(first, axis, down)


def exchange(value):
    return lax.all_to_all(value, "sub", split_axis=0, concat_axis=0, tiled=True)


def on_device(
    positions, velocities, mass, smoothing, energy, cell_counts, send_cells, partners, mig_list, mig_counts
):
    cells = mass.shape[0]
    peers = lax.axis_size("sub")
    kept = send_cells.shape[2]
    near_width = cells + 2
    full_width = near_width + peers * kept
    send = send_cells[0].T
    links = partners.T

    rec, first, last, outgoing = call(
        pack_kernel,
        [
            shape(cells, 8, HALF),
            shape(1, 8, HALF),
            shape(1, 8, HALF),
            shape(peers, 8 * kept, HALF),
        ],
        [cell_counts, send],
        [],
        [positions, mass],
        limit=60,
    )
    recv = exchange(outgoing)
    rim_lo, rim_hi = to_neighbours(first, last, "slab")

    keep = jnp.arange(M)[None, :] < mig_counts[0][:, None]
    picks = jnp.where(keep, mig_list[0], -P_SIZE).reshape(1, peers * M)

    def tables(width):
        return [
            pltpu.VMEM((width, 8, HALF), f32),
            pltpu.VMEM((width, K_ROWS, P_SIZE), bf16),
        ]

    def sums(size):
        return [
            pltpu.VMEM((size, P_SIZE, P_SIZE), f32),
            pltpu.VMEM((P_SIZE, HALF), f32),
            pltpu.VMEM((P_SIZE, HALF), f32),
            pltpu.VMEM((P_SIZE, HALF), bf16),
            pltpu.VMEM((P_SIZE, HALF), bf16),
        ]

    near, left, order = call(
        near_density_kernel,
        [
            shape(cells, P_SIZE),
            jax.ShapeDtypeStruct((cells, P_SIZE, HALF), bf16),
            jax.ShapeDtypeStruct((cells,), jnp.int32),
        ],
        [],
        [cell_counts],
        [rec, rim_lo, rim_hi, smoothing],
        tables(near_width) + [pltpu.SMEM((cells,), jnp.int32), pltpu.SemaphoreType.DMA] + sums(1),
    )
    density, press, press_rec, first, last, press_out = call(
        density_kernel,
        [
            shape(cells, P_SIZE),
            shape(cells, P_SIZE),
            shape(cells, 2, HALF),
            shape(1, 2, HALF),
            shape(1, 2, HALF),
            shape(peers, 2 * kept, HALF),
        ],
        [order, links],
        [send],
        [rec, rim_lo, rim_hi, recv, left, smoothing, energy, near],
        tables(full_width)
        + [pltpu.VMEM((cells, P_SIZE), f32), pltpu.SMEM((kept, peers), jnp.int32), pltpu.SemaphoreType.DMA]
        + sums(2),
    )
    press_recv = exchange(press_out)
    press_lo, press_hi = to_neighbours(first, last, "slab")

    def force_tables(width, slots):
        return tables(width) + [
            pltpu.VMEM((width, 2, HALF), f32),
            pltpu.VMEM((width, V_ROWS, P_SIZE), bf16),
            pltpu.VMEM((slots, P_SIZE, P_SIZE), f32),
            pltpu.VMEM((2, P_SIZE, P_SIZE), bf16),
            pltpu.VMEM((2, P_SIZE, P_SIZE), bf16),
            pltpu.VMEM((V_ROWS, P_SIZE), f32),
        ]

    (near,) = call(
        near_force_kernel,
        [shape(cells, 8, P_SIZE)],
        [order],
        [],
        [rec, rim_lo, rim_hi, left, press_rec, press_lo, press_hi],
        force_tables(near_width, 2),
    )
    state, leaving = call(
        force_kernel,
        [shape(6, cells, P_SIZE), shape(peers, HALF)],
        [order, links],
        [],
        [
            rec, rim_lo, rim_hi, recv, left, press_rec, press_lo, press_hi, press_recv,
            smoothing, positions, velocities, press, near, picks,
        ],
        force_tables(full_width, 3) + [pltpu.VMEM((8, cells, P_SIZE), f32)],
    )
    arrived = exchange(leaving.reshape(peers, 1, HALF)).reshape(peers, HALF)
    (arrivals,) = call(arrive_kernel, [shape(6, peers * M)], [], [], [arrived])
    return density, state, arrivals


def solution(mesh):
    both = ("slab", "sub")
    return jax.shard_map(
        on_device,
        mesh=mesh,
        in_specs=(
            P(None, both, None),
            P(None, both, None),
            P(both, None),
            P(both, None),
            P(both, None),
            P(both),
            P(both, None, None),
            P(both, None),
            P(both, None, None),
            P(both, None),
        ),
        out_specs=(P(both, None), P(None, both, None), P(None, both)),
        check_vma=False,
    )
```

```python
import functools
import math

import jax
import jax.numpy as jnp
from jax import lax
from jax.experimental import pallas as pl
from jax.experimental.pallas import tpu as pltpu
from jax.sharding import PartitionSpec as P

P_SIZE = 256
HALF = 128
M = 8
NEAR = 2
K_ROWS = 32
V_ROWS = 32
STEP = 16
SIZES = tuple(range(128, P_SIZE + 1, STEP))
TINY = 1e-12
MASS_SCALE = 1024.0

adiabatic = 5.0 / 3.0
time_step = 0.05

f32 = jnp.float32
bf16 = jnp.bfloat16
VMEM = pl.BlockSpec(memory_space=pltpu.VMEM)
SMEM = pl.BlockSpec(memory_space=pltpu.SMEM)
HBM = pl.BlockSpec(memory_space=pl.ANY)
LAST = (((1,), (1,)), ((), ()))
FIRST = (((0,), (0,)), ((), ()))


def dot(a, b, dims=(((1,), (0,)), ((), ()))):
    return lax.dot_general(a, b, dims, preferred_element_type=f32)


def shape(*dims):
    return jax.ShapeDtypeStruct(dims, f32)


def split(value):
    high = value.astype(bf16).astype(f32)
    rest = value - high
    mid = rest.astype(bf16).astype(f32)
    return high, mid, rest - mid


def row_ids():
    return lax.broadcasted_iota(jnp.int32, (8, HALF), 0)


def lanes():
    return lax.broadcasted_iota(jnp.int32, (1, P_SIZE), 1)


def live_slots(rec):
    rows = [
        jnp.concatenate([rec[c, 3:4, :], rec[c, 7:8, :]], axis=1) for c in range(rec.shape[0])
    ]
    return jnp.concatenate(rows, axis=0) > 0.0


def swap(tile):
    return pltpu.roll(tile, 4, 0)


def is_fourth():
    return row_ids() % 4 == 3


def norms(tile):
    square = tile * tile
    return pltpu.roll(square, 1, 0) + pltpu.roll(square, 2, 0) + pltpu.roll(square, 3, 0)


def spread_fourth(tile):
    tile = jnp.where(is_fourth(), tile, 0.0)
    tile = tile + pltpu.roll(tile, 7, 0)
    return tile + pltpu.roll(tile, 6, 0)


def halves(first, second):
    top = row_ids() < 4
    return jnp.where(top, first, swap(second)), jnp.where(top, swap(first), second)


def by_row(parts):
    rows = row_ids()
    tile = 0.0
    for k, part in reversed(list(enumerate(parts))):
        tile = jnp.where(rows == k, part, tile)
    return tile


def right_operand(record, weighted):
    rows = row_ids()
    feature = jnp.where(is_fourth(), norms(record), record)
    if weighted:
        root = spread_fourth(record)
        feature = feature * (root * root)
    high, mid, low = split(feature)
    tiles = [halves(high, high), halves(mid, high), halves(low, mid)]
    if weighted:
        ones = []
        for value in halves(root * root, root * root):
            h, m, l = split(value)
            ones.append(jnp.where(rows < 3, h, jnp.where(rows < 5, m, jnp.where(rows < 6, l, 0.0))))
    else:
        ones = [jnp.where(rows < 3, 1.0, 0.0)] * 2
    parts = [jnp.concatenate([tile[k] for tile in tiles] + [ones[k]], axis=0) for k in range(2)]
    return jnp.concatenate(parts, axis=1).astype(bf16)


def left_operand(record, width):
    scale = 1.0 / (width * width)
    scale = jnp.where(row_ids() < 4, scale[:, :HALF], scale[:, HALF:])
    feature = scale * jnp.where(is_fourth(), 1.0, -2.0 * record)
    high, mid, low = split(feature)
    first, second = halves(high, mid), halves(high, low)
    own = spread_fourth(scale * norms(record))
    parts = []
    for k, value in enumerate(halves(own, own)):
        h, m, l = split(value)
        one = by_row([h, m, l, h, m, h])
        pad = jnp.zeros((HALF - K_ROWS, HALF), f32)
        parts.append(jnp.concatenate([first[k], second[k], first[k], one, pad], axis=0).T)
    return jnp.concatenate(parts, axis=0).astype(bf16)


def weight_operand(record, press):
    root = spread_fourth(record)
    plain = jnp.where(is_fourth(), 1.0, record) * (root * root * root * (1.0 / MASS_SCALE))
    pressed = plain * jnp.where(row_ids() < 4, press[0:1, :], press[1:2, :])
    tiles = [halves(*pair) for pair in zip(split(plain), split(pressed))]
    blank = jnp.zeros((8, HALF), f32)
    parts = [jnp.concatenate([tile[k] for tile in tiles] + [blank], axis=0) for k in range(2)]
    return jnp.concatenate(parts, axis=1).astype(bf16)


def sort_cells(counts, order):
    cells = order.shape[0]
    keys = []
    for c in range(cells):
        kind = jnp.maximum(lax.div(counts[c] + (STEP - 1), STEP) - SIZES[0] // STEP, 0)
        keys.append(kind * cells + c)
    places = [cells - 1 - c for c in range(cells)]
    for c in range(cells):
        for other in range(c + 1, cells):
            behind = (keys[c] > keys[other]).astype(jnp.int32)
            places[c] = places[c] + (behind - 1)
            places[other] = places[other] + (1 - behind)
    for c in range(cells):
        order[places[c]] = keys[c]


def pack_kernel(counts, send, pos, mass, rec, first, last, out):
    cells = mass.shape[0]
    scaled = mass[...] * MASS_SCALE
    root = jnp.exp(jnp.log(scaled) * (1.0 / 3.0))
    for _ in range(2):
        root = root - (root * root * root - scaled) / (3.0 * root * root)
    for c in range(cells):
        live = lanes() < counts[c]
        for k in range(4):
            row = pos[k, c : c + 1, :] - 0.5 if k < 3 else root[c : c + 1, :]
            row = jnp.where(live, row, 0.0)
            rec[c, k : k + 1, :] = row[:, :HALF]
            rec[c, k + 4 : k + 5, :] = row[:, HALF:]
    first[0] = rec[0]
    last[0] = rec[cells - 1]
    for v in range(out.shape[0]):
        for k in range(send.shape[0]):
            out[v, 8 * k : 8 * k + 8, :] = rec[send[k, v]]


def fill_table(table, rec, rim_lo, rim_hi, recv, rows):
    cells = rec.shape[0]
    table[0] = rim_lo[0]
    for c in range(cells):
        table[1 + c] = rec[c]
    table[cells + 1] = rim_hi[0]
    if recv is not None:
        per_peer = recv.shape[1] // rows
        for v in range(recv.shape[0]):
            for k in range(per_peer):
                table[cells + 2 + v * per_peer + k] = recv[v, rows * k : rows * k + rows, :]


def for_cells(count, step):
    unroll = 4
    done = count - count % unroll

    def body(t, carry):
        step(t)
        return carry

    lax.fori_loop(0, done, body, 0, unroll=unroll)
    for t in range(done, count):
        step(t)


def fill_left(rec, smoothing, left):
    for c in range(rec.shape[0]):
        left[c] = left_operand(rec[c], smoothing[c : c + 1, :])


def cell_at(order, n):
    cells = order.shape[0]
    return lax.rem(order[jnp.clip(n, 0, cells - 1)], cells)


def by_size(order, run):
    cells = order.shape[0]
    done = jnp.int32(0)
    for k, size in enumerate(SIZES):

        def more(n, k=k):
            return (n < cells) & (order[jnp.minimum(n, cells - 1)] < (k + 1) * cells)

        def step(n, size=size):
            run(cell_at(order, n), cell_at(order, n - 1), cell_at(order, n + 1), size)
            return n + 1

        done = lax.while_loop(more, step, done)


def density_sums(
    order, partners, groups, table, right, left, square, total, inner_total, value_high, value_low, store
):
    slots = len(groups)

    def product(c, g, size):
        for k, p in enumerate(groups[g]):
            square[k, :size, :] = jnp.maximum(dot(left[c, :size, :K_ROWS], right[partners[p, c]]), TINY)

    def reduce():
        ones = jnp.ones((8, HALF), bf16)
        return (dot(ones, value_high[...], LAST) + dot(ones, value_low[...], LAST))[0:1, :]

    def run(c, before, after, size):
        for g, group in enumerate(groups):
            if g == 0:
                store(before, reduce())
            roots = [table[partners[p, c], r : r + 1, :] for p in group for r in (3, 7)]
            doubled = [root + root for root in roots]
            for base in range(0, size, STEP):
                block = pl.ds(base, STEP)
                outer_sum = inner_sum = None
                for k in range(len(roots)):
                    half = slice((k % 2) * HALF, (k % 2 + 1) * HALF)
                    s = square[k // 2, block, half]
                    outer = jnp.maximum(doubled[k] - s * lax.rsqrt(s), 0.0)
                    inner = jnp.maximum(outer - roots[k], 0.0)
                    outer = outer * outer * outer
                    inner = inner * inner * inner
                    outer_sum = outer if k == 0 else outer_sum + outer
                    inner_sum = inner if k == 0 else inner_sum + inner
                if g:
                    outer_sum = total[block, :] + outer_sum
                    inner_sum = inner_total[block, :] + inner_sum
                if g + 1 < slots:
                    total[block, :] = outer_sum
                    inner_total[block, :] = inner_sum
                else:
                    value = 0.25 * outer_sum - inner_sum
                    high = value.astype(bf16)
                    value_high[block, :] = high
                    value_low[block, :] = (value - high.astype(f32)).astype(bf16)
            if g + 1 < slots:
                product(c, g + 1, size)
            else:
                product(after, 0, P_SIZE)

    product(cell_at(order, 0), 0, P_SIZE)
    by_size(order, run)
    store(cell_at(order, order.shape[0] - 1), reduce())


def begin(*copies):
    started = [pltpu.make_async_copy(*copy) for copy in copies]
    for copy in started:
        copy.start()
    return started


def finish_all(started):
    for copy in started:
        copy.wait()


class near_partners:
    def __init__(self, cells):
        self.cells = cells

    def __getitem__(self, place):
        p, c = place
        return c + 1 if p == 0 else jnp.where(c < self.cells // 2, 0, self.cells + 1)


def near_density_kernel(
    counts_ref, rec, rim_lo, rim_hi, smoothing, sums, left, order, table, right, counts, copied, *scratch
):
    copy = pltpu.make_async_copy(counts_ref, counts, copied)
    copy.start()
    fill_table(table, rec, rim_lo, rim_hi, None, 8)
    fill_left(rec, smoothing, left)

    def step(t):
        right[t] = right_operand(table[t], True)

    for_cells(table.shape[0], step)
    copy.wait()
    sort_cells(counts, order)

    def store(c, row):
        sums[pl.ds(c, 1), :] = row

    density_sums(order, near_partners(rec.shape[0]), [(0,), (1,)], table, right, left, *scratch, store)


def density_kernel(
    order_ref, partners_ref, send_ref, rec, rim_lo, rim_hi, recv, left, smoothing, energy, near,
    density_ref, press, press_rec, first, last, press_send,
    table, right, sums, density, order, partners, send, copied, *scratch,
):
    cells = rec.shape[0]
    lists = begin(
        (order_ref, order, copied.at[0]), (partners_ref, partners, copied.at[1]), (send_ref, send, copied.at[2])
    )
    fill_table(table, rec, rim_lo, rim_hi, recv, 8)

    def step(t):
        right[t] = right_operand(table[t], True)

    for_cells(table.shape[0], step)
    finish_all(lists)

    def store(c, row):
        sums[pl.ds(c, 1), :] = row

    pairs = partners.shape[0]
    groups = [tuple(range(p, min(p + 2, pairs))) for p in range(NEAR, pairs, 2)]
    density_sums(order, partners, groups, table, right, left, *scratch, store)
    width = smoothing[...]
    live = live_slots(rec)
    rho = (near[...] + sums[...]) * (1.0 / MASS_SCALE) / (math.pi * width * width * width)
    density[...] = jnp.where(live, rho, 0.0)
    stored = begin((density, density_ref, copied.at[3]))
    value = jnp.where(live, (adiabatic - 1.0) * energy[...] / jnp.where(live, rho, 1.0), 0.0)
    press[...] = value
    for c in range(cells):
        press_rec[c, 0:1, :] = value[c : c + 1, :HALF]
        press_rec[c, 1:2, :] = value[c : c + 1, HALF:]
    first[0] = press_rec[0]
    last[0] = press_rec[cells - 1]
    for v in range(send.shape[1]):
        for k in range(send.shape[0]):
            press_send[v, 2 * k : 2 * k + 2, :] = press_rec[send[k, v]]
    finish_all(stored)


def force_sums(
    order, partners, columns, right, left, weights, square, slope_high, slope_low, total, store
):
    count = len(columns)
    slots = square.shape[0]
    ahead = slots - 1

    def product(c, n, size):
        square[n % slots, :size, :] = jnp.minimum(jnp.maximum(dot(left[c, :size, :K_ROWS], right[partners[columns[n], c]]), TINY), 4.0)

    def gather(c, n, size):
        w = weights[partners[columns[n], c]]
        return dot(w, slope_high[n % 2, :size, :], LAST) + dot(w, slope_low[n % 2, :size, :], LAST)

    def finish(c):
        found = total[...] + gather(c, count - 1, P_SIZE)
        store(c, found[0:8, :] + found[8:16, :] + found[16:24, :])

    def run(c, before, after, size):
        added = None
        for n in range(count):
            if n + ahead < count:
                product(c, n + ahead, size)
            else:
                product(after, n + ahead - count, P_SIZE)
            if n == 0:
                finish(before)
            else:
                more = gather(c, n - 1, size)
                added = more if n == 1 else added + more
            for base in range(0, size, STEP):
                block = pl.ds(base, STEP)
                s = square[n % slots, block, :]
                y = lax.rsqrt(s)
                q = s * y
                f = (jnp.minimum(y, 1.0) - 1.0) + (jnp.maximum(q, 1.0) - 0.75 * q)
                high = f.astype(bf16)
                slope_high[n % 2, block, :] = high
                slope_low[n % 2, block, :] = (f - high.astype(f32)).astype(bf16)
        total[:, :size] = added

    for n in range(ahead):
        product(cell_at(order, 0), n, P_SIZE)
    by_size(order, run)
    finish(cell_at(order, order.shape[0] - 1))


def near_force_kernel(
    order_ref, rec, rim_lo, rim_hi, left, press_rec, press_lo, press_hi, sums,
    order, copied, table, right, press_table, weights, square, slope_high, slope_low, total,
):
    lists = begin((order_ref, order, copied.at[0]))
    fill_table(table, rec, rim_lo, rim_hi, None, 8)
    fill_table(press_table, press_rec, press_lo, press_hi, None, 2)

    def step(t):
        right[t] = right_operand(table[t], False)
        weights[t] = weight_operand(table[t], press_table[t])

    for_cells(table.shape[0], step)
    finish_all(lists)

    def store(c, found):
        sums[c] = found

    force_sums(
        order, near_partners(rec.shape[0]), list(range(NEAR)), right, left, weights, square, slope_high, slope_low, total, store
    )


def slot_maps(slots, peers):
    block = lax.broadcasted_iota(jnp.int32, (peers, slots), 1) // M
    owner = (block == lax.broadcasted_iota(jnp.int32, (peers, slots), 0)).astype(f32).astype(bf16)
    column = lax.broadcasted_iota(jnp.int32, (slots, HALF), 1)
    slot = lax.broadcasted_iota(jnp.int32, (slots, HALF), 0)
    return owner, column % M == slot % M


def field_map():
    field = lax.broadcasted_iota(jnp.int32, (8, HALF), 1) // M
    return (field == lax.broadcasted_iota(jnp.int32, (8, HALF), 0)).astype(f32)


def force_kernel(
    order_ref, partners_ref, rec, rim_lo, rim_hi, recv, left, press_rec, press_lo, press_hi, press_recv,
    smoothing, pos, vel, press, near, picks,
    state_ref, leaving,
    state, order, partners, copied, table, right, press_table, weights, square, slope_high, slope_low, total, sums,
):
    cells = rec.shape[0]
    lists = begin((order_ref, order, copied.at[0]), (partners_ref, partners, copied.at[1]))
    fill_table(table, rec, rim_lo, rim_hi, recv, 8)
    fill_table(press_table, press_rec, press_lo, press_hi, press_recv, 2)

    def step(t):
        right[t] = right_operand(table[t], False)
        weights[t] = weight_operand(table[t], press_table[t])

    for_cells(table.shape[0], step)
    finish_all(lists)

    def store(c, found):
        found = near[c] + found
        for k in range(8):
            sums[k, pl.ds(c, 1), :] = found[k : k + 1, :]

    force_sums(
        order, partners, list(range(NEAR, partners.shape[0])), right, left, weights, square,
        slope_high, slope_low, total, store,
    )

    width = smoothing[...]
    squared = width * width
    factor = (3.0 * time_step / math.pi) / (squared * squared * width)
    own = press[...]
    live = live_slots(rec)
    for k in range(3):
        place = pos[k]
        centred = place - 0.5
        push = own * (centred * sums[3] - sums[k]) + (centred * sums[7] - sums[4 + k])
        speed = vel[k] + factor * push
        state[k] = jnp.where(live, place + time_step * speed, 0.0)
        state[3 + k] = jnp.where(live, speed, 0.0)

    stored = begin((state, state_ref, copied.at[2]))
    slots = picks.shape[1]
    picked = picks[...]
    chosen = lax.broadcasted_iota(jnp.int32, (P_SIZE, slots), 0) == picked % P_SIZE
    chosen = chosen.astype(f32).astype(bf16)
    mine = lax.broadcasted_iota(jnp.int32, (cells, slots), 0) == picked // P_SIZE
    parts = [split(state[k]) for k in range(6)]
    parts = jnp.concatenate([part[n] for n in range(3) for part in parts], axis=0).astype(bf16)
    found = dot(parts, chosen)
    rows = []
    for k in range(6):
        value = sum(found[(6 * n + k) * cells : (6 * n + k + 1) * cells, :] for n in range(3))
        rows.append(jnp.sum(jnp.where(mine, value, 0.0), axis=0, keepdims=True))
    found = jnp.concatenate(rows + [jnp.zeros((2, slots), f32)], axis=0)
    owner, same = slot_maps(slots, leaving.shape[0])
    spread = field_map()
    blank = jnp.zeros_like(spread)
    spread = jnp.concatenate(
        [jnp.concatenate([spread if n == k else blank for n in range(3)], axis=1) for k in range(3)], axis=0
    )
    wide = dot(jnp.concatenate(split(found), axis=0).astype(bf16), spread.astype(bf16), FIRST)
    wide = jnp.concatenate(
        [jnp.where(same, wide[:, HALF * n : HALF * (n + 1)], 0.0) for n in range(3)], axis=1
    )
    value = dot(owner, wide.astype(bf16))
    leaving[...] = sum(value[:, HALF * n : HALF * (n + 1)] for n in range(3))
    finish_all(stored)


def arrive_kernel(arrived, out):
    owner, same = slot_maps(out.shape[1], arrived.shape[0])
    wide = dot(owner, jnp.concatenate(split(arrived[...]), axis=1).astype(bf16), FIRST)
    wide = jnp.concatenate(
        [jnp.where(same, wide[:, HALF * n : HALF * (n + 1)], 0.0) for n in range(3)], axis=1
    )
    spread = field_map()
    value = dot(jnp.concatenate([spread] * 3, axis=1).astype(bf16), wide.astype(bf16), LAST)
    out[...] = value[: out.shape[0], :]


def call(kernel, outs, smem, hbm, vmem, scratch=(), limit=48, direct=()):
    return pl.pallas_call(
        kernel,
        out_shape=tuple(outs),
        in_specs=[SMEM] * len(smem) + [HBM] * len(hbm) + [VMEM] * len(vmem),
        out_specs=tuple(
            HBM if n in direct else SMEM if out.dtype == jnp.int32 else VMEM for n, out in enumerate(outs)
        ),
        scratch_shapes=scratch,
        compiler_params=pltpu.CompilerParams(vmem_limit_bytes=limit * 1024 * 1024),
    )(*smem, *hbm, *vmem)


def to_neighbours(first, last, axis):
    count = lax.axis_size(axis)
    up = [(i, (i + 1) % count) for i in range(count)]
    down = [(j, i) for i, j in up]
    return lax.ppermute(last, axis, up), lax.ppermute(first, axis, down)


def exchange(value):
    return lax.all_to_all(value, "sub", split_axis=0, concat_axis=0, tiled=True)


def on_device(
    positions, velocities, mass, smoothing, energy, cell_counts, send_cells, partners, mig_list, mig_counts
):
    cells = mass.shape[0]
    peers = lax.axis_size("sub")
    kept = send_cells.shape[2]
    near_width = cells + 2
    full_width = near_width + peers * kept
    send = send_cells[0].T
    links = partners.T

    rec, first, last, outgoing = call(
        pack_kernel,
        [
            shape(cells, 8, HALF),
            shape(1, 8, HALF),
            shape(1, 8, HALF),
            shape(peers, 8 * kept, HALF),
        ],
        [cell_counts, send],
        [],
        [positions, mass],
        limit=60,
    )
    recv = exchange(outgoing)
    rim_lo, rim_hi = to_neighbours(first, last, "slab")

    keep = jnp.arange(M)[None, :] < mig_counts[0][:, None]
    picks = jnp.where(keep, mig_list[0], -P_SIZE).reshape(1, peers * M)

    def tables(width):
        return [
            pltpu.VMEM((width, 8, HALF), f32),
            pltpu.VMEM((width, K_ROWS, P_SIZE), bf16),
        ]

    def sums(size):
        return [
            pltpu.VMEM((size, P_SIZE, P_SIZE), f32),
            pltpu.VMEM((P_SIZE, HALF), f32),
            pltpu.VMEM((P_SIZE, HALF), f32),
            pltpu.VMEM((P_SIZE, HALF), bf16),
            pltpu.VMEM((P_SIZE, HALF), bf16),
        ]

    near, left, order = call(
        near_density_kernel,
        [
            shape(cells, P_SIZE),
            jax.ShapeDtypeStruct((cells, P_SIZE, HALF), bf16),
            jax.ShapeDtypeStruct((cells,), jnp.int32),
        ],
        [],
        [cell_counts],
        [rec, rim_lo, rim_hi, smoothing],
        tables(near_width) + [pltpu.SMEM((cells,), jnp.int32), pltpu.SemaphoreType.DMA] + sums(1),
    )
    density, press, press_rec, first, last, press_out = call(
        density_kernel,
        [
            shape(cells, P_SIZE),
            shape(cells, P_SIZE),
            shape(cells, 2, HALF),
            shape(1, 2, HALF),
            shape(1, 2, HALF),
            shape(peers, 2 * kept, HALF),
        ],
        [],
        [order, links, send],
        [rec, rim_lo, rim_hi, recv, left, smoothing, energy, near],
        tables(full_width)
        + [pltpu.VMEM((cells, P_SIZE), f32), pltpu.VMEM((cells, P_SIZE), f32)]
        + [pltpu.SMEM((cells,), jnp.int32), pltpu.SMEM(links.shape, jnp.int32), pltpu.SMEM(send.shape, jnp.int32)]
        + [pltpu.SemaphoreType.DMA((4,))]
        + sums(2),
        direct=(0,),
    )
    press_recv = exchange(press_out)
    press_lo, press_hi = to_neighbours(first, last, "slab")

    def force_tables(width, slots):
        return tables(width) + [
            pltpu.VMEM((width, 2, HALF), f32),
            pltpu.VMEM((width, V_ROWS, P_SIZE), bf16),
            pltpu.VMEM((slots, P_SIZE, P_SIZE), f32),
            pltpu.VMEM((2, P_SIZE, P_SIZE), bf16),
            pltpu.VMEM((2, P_SIZE, P_SIZE), bf16),
            pltpu.VMEM((V_ROWS, P_SIZE), f32),
        ]

    (near,) = call(
        near_force_kernel,
        [shape(cells, 8, P_SIZE)],
        [],
        [order],
        [rec, rim_lo, rim_hi, left, press_rec, press_lo, press_hi],
        [pltpu.SMEM((cells,), jnp.int32), pltpu.SemaphoreType.DMA((1,))] + force_tables(near_width, 2),
    )
    state, leaving = call(
        force_kernel,
        [shape(6, cells, P_SIZE), shape(peers, HALF)],
        [],
        [order, links],
        [
            rec, rim_lo, rim_hi, recv, left, press_rec, press_lo, press_hi, press_recv,
            smoothing, positions, velocities, press, near, picks,
        ],
        [pltpu.VMEM((6, cells, P_SIZE), f32), pltpu.SMEM((cells,), jnp.int32), pltpu.SMEM(links.shape, jnp.int32)]
        + [pltpu.SemaphoreType.DMA((3,))]
        + force_tables(full_width, 3)
        + [pltpu.VMEM((8, cells, P_SIZE), f32)],
        direct=(0,),
    )
    arrived = exchange(leaving.reshape(peers, 1, HALF)).reshape(peers, HALF)
    (arrivals,) = call(arrive_kernel, [shape(6, peers * M)], [], [], [arrived])
    return density, state, arrivals


def solution(mesh):
    both = ("slab", "sub")
    return jax.shard_map(
        on_device,
        mesh=mesh,
        in_specs=(
            P(None, both, None),
            P(None, both, None),
            P(both, None),
            P(both, None),
            P(both, None),
            P(both),
            P(both, None, None),
            P(both, None),
            P(both, None, None),
            P(both, None),
        ),
        out_specs=(P(both, None), P(None, both, None), P(None, both)),
        check_vma=False,
    )
```

```python
import functools
import math

import jax
import jax.numpy as jnp
from jax import lax
from jax.experimental import pallas as pl
from jax.experimental.pallas import tpu as pltpu
from jax.sharding import PartitionSpec as P

P_SIZE = 256
HALF = 128
M = 8
NEAR = 2
K_ROWS = 32
V_ROWS = 32
STEP = 16
SIZES = tuple(range(128, P_SIZE + 1, STEP))
TINY = 1e-12
MASS_SCALE = 1024.0

adiabatic = 5.0 / 3.0
time_step = 0.05

f32 = jnp.float32
bf16 = jnp.bfloat16
VMEM = pl.BlockSpec(memory_space=pltpu.VMEM)
SMEM = pl.BlockSpec(memory_space=pltpu.SMEM)
HBM = pl.BlockSpec(memory_space=pl.ANY)
LAST = (((1,), (1,)), ((), ()))
FIRST = (((0,), (0,)), ((), ()))


def dot(a, b, dims=(((1,), (0,)), ((), ()))):
    return lax.dot_general(a, b, dims, preferred_element_type=f32)


def shape(*dims):
    return jax.ShapeDtypeStruct(dims, f32)


def split(value):
    high = value.astype(bf16).astype(f32)
    rest = value - high
    mid = rest.astype(bf16).astype(f32)
    return high, mid, rest - mid


def row_ids():
    return lax.broadcasted_iota(jnp.int32, (8, HALF), 0)


def lanes():
    return lax.broadcasted_iota(jnp.int32, (1, P_SIZE), 1)


def live_slots(rec):
    rows = [
        jnp.concatenate([rec[c, 3:4, :], rec[c, 7:8, :]], axis=1) for c in range(rec.shape[0])
    ]
    return jnp.concatenate(rows, axis=0) > 0.0


def swap(tile):
    return pltpu.roll(tile, 4, 0)


def is_fourth():
    return row_ids() % 4 == 3


def norms(tile):
    square = tile * tile
    return pltpu.roll(square, 1, 0) + pltpu.roll(square, 2, 0) + pltpu.roll(square, 3, 0)


def spread_fourth(tile):
    tile = jnp.where(is_fourth(), tile, 0.0)
    tile = tile + pltpu.roll(tile, 7, 0)
    return tile + pltpu.roll(tile, 6, 0)


def halves(first, second):
    top = row_ids() < 4
    return jnp.where(top, first, swap(second)), jnp.where(top, swap(first), second)


def by_row(parts):
    rows = row_ids()
    tile = 0.0
    for k, part in reversed(list(enumerate(parts))):
        tile = jnp.where(rows == k, part, tile)
    return tile


def right_operand(record, weighted):
    rows = row_ids()
    feature = jnp.where(is_fourth(), norms(record), record)
    if weighted:
        root = spread_fourth(record)
        feature = feature * (root * root)
    high, mid, low = split(feature)
    tiles = [halves(high, high), halves(mid, high), halves(low, mid)]
    if weighted:
        ones = []
        for value in halves(root * root, root * root):
            h, m, l = split(value)
            ones.append(jnp.where(rows < 3, h, jnp.where(rows < 5, m, jnp.where(rows < 6, l, 0.0))))
    else:
        ones = [jnp.where(rows < 3, 1.0, 0.0)] * 2
    parts = [jnp.concatenate([tile[k] for tile in tiles] + [ones[k]], axis=0) for k in range(2)]
    return jnp.concatenate(parts, axis=1).astype(bf16)


def left_operand(record, width):
    scale = 1.0 / (width * width)
    scale = jnp.where(row_ids() < 4, scale[:, :HALF], scale[:, HALF:])
    feature = scale * jnp.where(is_fourth(), 1.0, -2.0 * record)
    high, mid, low = split(feature)
    first, second = halves(high, mid), halves(high, low)
    own = spread_fourth(scale * norms(record))
    parts = []
    for k, value in enumerate(halves(own, own)):
        h, m, l = split(value)
        one = by_row([h, m, l, h, m, h])
        pad = jnp.zeros((HALF - K_ROWS, HALF), f32)
        parts.append(jnp.concatenate([first[k], second[k], first[k], one, pad], axis=0).T)
    return jnp.concatenate(parts, axis=0).astype(bf16)


def weight_operand(record, press):
    root = spread_fourth(record)
    plain = jnp.where(is_fourth(), 1.0, record) * (root * root * root * (1.0 / MASS_SCALE))
    pressed = plain * jnp.where(row_ids() < 4, press[0:1, :], press[1:2, :])
    tiles = [halves(*pair) for pair in zip(split(plain), split(pressed))]
    blank = jnp.zeros((8, HALF), f32)
    parts = [jnp.concatenate([tile[k] for tile in tiles] + [blank], axis=0) for k in range(2)]
    return jnp.concatenate(parts, axis=1).astype(bf16)


def sort_cells(counts, order):
    cells = order.shape[0]
    keys = []
    for c in range(cells):
        kind = jnp.maximum(lax.div(counts[c] + (STEP - 1), STEP) - SIZES[0] // STEP, 0)
        keys.append(kind * cells + c)
    places = [cells - 1 - c for c in range(cells)]
    for c in range(cells):
        for other in range(c + 1, cells):
            behind = (keys[c] > keys[other]).astype(jnp.int32)
            places[c] = places[c] + (behind - 1)
            places[other] = places[other] + (1 - behind)
    for c in range(cells):
        order[places[c]] = keys[c]


def pack_kernel(counts, send, pos, mass, rec, first, last, out):
    cells = mass.shape[0]
    scaled = mass[...] * MASS_SCALE
    root = jnp.exp(jnp.log(scaled) * (1.0 / 3.0))
    for _ in range(2):
        root = root - (root * root * root - scaled) / (3.0 * root * root)
    for c in range(cells):
        live = lanes() < counts[c]
        for k in range(4):
            row = pos[k, c : c + 1, :] - 0.5 if k < 3 else root[c : c + 1, :]
            row = jnp.where(live, row, 0.0)
            rec[c, k : k + 1, :] = row[:, :HALF]
            rec[c, k + 4 : k + 5, :] = row[:, HALF:]
    first[0] = rec[0]
    last[0] = rec[cells - 1]
    for v in range(out.shape[0]):
        for k in range(send.shape[0]):
            out[v, 8 * k : 8 * k + 8, :] = rec[send[k, v]]


def fill_table(table, rec, rim_lo, rim_hi, recv, rows):
    cells = rec.shape[0]
    table[0] = rim_lo[0]
    for c in range(cells):
        table[1 + c] = rec[c]
    table[cells + 1] = rim_hi[0]
    if recv is not None:
        per_peer = recv.shape[1] // rows
        for v in range(recv.shape[0]):
            for k in range(per_peer):
                table[cells + 2 + v * per_peer + k] = recv[v, rows * k : rows * k + rows, :]


def for_cells(count, step):
    unroll = 4
    done = count - count % unroll

    def body(t, carry):
        step(t)
        return carry

    lax.fori_loop(0, done, body, 0, unroll=unroll)
    for t in range(done, count):
        step(t)


def fill_left(rec, smoothing, left):
    for c in range(rec.shape[0]):
        left[c] = left_operand(rec[c], smoothing[c : c + 1, :])


def cell_at(order, n):
    cells = order.shape[0]
    return lax.rem(order[jnp.clip(n, 0, cells - 1)], cells)


def by_size(order, run):
    cells = order.shape[0]
    done = jnp.int32(0)
    for k, size in enumerate(SIZES):

        def more(n, k=k):
            return (n < cells) & (order[jnp.minimum(n, cells - 1)] < (k + 1) * cells)

        def step(n, size=size):
            run(cell_at(order, n), cell_at(order, n - 1), cell_at(order, n + 1), size)
            return n + 1

        done = lax.while_loop(more, step, done)


def density_sums(
    order, partners, groups, table, right, left, square, total, inner_total, value_high, value_low, store
):
    slots = len(groups)

    def product(c, g, size):
        for k, p in enumerate(groups[g]):
            square[k, :size, :] = jnp.maximum(dot(left[c, :size, :K_ROWS], right[partners[p, c]]), TINY)

    def reduce():
        ones = jnp.ones((8, HALF), bf16)
        return (dot(ones, value_high[...], LAST) + dot(ones, value_low[...], LAST))[0:1, :]

    def run(c, before, after, size):
        for g, group in enumerate(groups):
            if g == 0:
                store(before, reduce())
            roots = [table[partners[p, c], r : r + 1, :] for p in group for r in (3, 7)]
            doubled = [root + root for root in roots]
            for base in range(0, size, STEP):
                block = pl.ds(base, STEP)
                outer_sum = inner_sum = None
                for k in range(len(roots)):
                    half = slice((k % 2) * HALF, (k % 2 + 1) * HALF)
                    s = square[k // 2, block, half]
                    outer = jnp.maximum(doubled[k] - s * lax.rsqrt(s), 0.0)
                    inner = jnp.maximum(outer - roots[k], 0.0)
                    outer = outer * outer * outer
                    inner = inner * inner * inner
                    outer_sum = outer if k == 0 else outer_sum + outer
                    inner_sum = inner if k == 0 else inner_sum + inner
                if g:
                    outer_sum = total[block, :] + outer_sum
                    inner_sum = inner_total[block, :] + inner_sum
                if g + 1 < slots:
                    total[block, :] = outer_sum
                    inner_total[block, :] = inner_sum
                else:
                    value = 0.25 * outer_sum - inner_sum
                    high = value.astype(bf16)
                    value_high[block, :] = high
                    value_low[block, :] = (value - high.astype(f32)).astype(bf16)
            if g + 1 < slots:
                product(c, g + 1, size)
            else:
                product(after, 0, P_SIZE)

    product(cell_at(order, 0), 0, P_SIZE)
    by_size(order, run)
    store(cell_at(order, order.shape[0] - 1), reduce())


def begin(*copies):
    started = [pltpu.make_async_copy(*copy) for copy in copies]
    for copy in started:
        copy.start()
    return started


def finish_all(started):
    for copy in started:
        copy.wait()


class near_partners:
    def __init__(self, cells):
        self.cells = cells

    def __getitem__(self, place):
        p, c = place
        return c + 1 if p == 0 else jnp.where(c < self.cells // 2, 0, self.cells + 1)


class Indexed:
    def __init__(self, function):
        self.function = function

    def __getitem__(self, place):
        return self.function(*place)


def operands_kernel(counts_ref, send_ref, rec, smoothing, left, right, order, counts, copied):
    del send_ref
    lists = begin((counts_ref, counts, copied.at[0]))
    fill_left(rec, smoothing, left)

    def step(t):
        right[t] = right_operand(rec[t], True)

    for_cells(rec.shape[0], step)
    finish_all(lists)
    sort_cells(counts, order)


def near_density_kernel(order_ref, rec, rim_lo, rim_hi, left, own, sums, order, copied, table, right, *scratch):
    lists = begin((order_ref, order, copied.at[0]))
    cells = rec.shape[0]
    for t, rim in enumerate((rim_lo, rim_hi)):
        table[t] = rim[0]
        right[t] = right_operand(rim[0], True)

    def side(c):
        return (c >= cells // 2).astype(jnp.int32)

    def store(c, row):
        sums[pl.ds(c, 1), :] = row

    finish_all(lists)
    density_sums(
        order,
        Indexed(lambda p, c: (p, c)),
        [(0,), (1,)],
        Indexed(lambda at, *rest: table[(side(at[1]), *rest)] if at[0] else rec[(at[1], *rest)]),
        Indexed(lambda p, c: right[side(c)] if p else own[c]),
        left,
        *scratch,
        store,
    )


def density_kernel(
    order_ref, partners_ref, send_ref, rec, rim_lo, rim_hi, recv, left, smoothing, energy, near,
    density_ref, press, press_rec, first, last, press_send,
    table, right, sums, density, order, partners, send, copied, *scratch,
):
    cells = rec.shape[0]
    lists = begin(
        (order_ref, order, copied.at[0]), (partners_ref, partners, copied.at[1]), (send_ref, send, copied.at[2])
    )
    fill_table(table, rec, rim_lo, rim_hi, recv, 8)

    def step(t):
        right[t] = right_operand(table[t], True)

    for_cells(table.shape[0], step)
    finish_all(lists)

    def store(c, row):
        sums[pl.ds(c, 1), :] = row

    pairs = partners.shape[0]
    groups = [tuple(range(p, min(p + 2, pairs))) for p in range(NEAR, pairs, 2)]
    density_sums(order, partners, groups, table, right, left, *scratch, store)
    width = smoothing[...]
    live = live_slots(rec)
    rho = (near[...] + sums[...]) * (1.0 / MASS_SCALE) / (math.pi * width * width * width)
    density[...] = jnp.where(live, rho, 0.0)
    stored = begin((density, density_ref, copied.at[3]))
    value = jnp.where(live, (adiabatic - 1.0) * energy[...] / jnp.where(live, rho, 1.0), 0.0)
    press[...] = value
    for c in range(cells):
        press_rec[c, 0:1, :] = value[c : c + 1, :HALF]
        press_rec[c, 1:2, :] = value[c : c + 1, HALF:]
    first[0] = press_rec[0]
    last[0] = press_rec[cells - 1]
    for v in range(send.shape[1]):
        for k in range(send.shape[0]):
            press_send[v, 2 * k : 2 * k + 2, :] = press_rec[send[k, v]]
    finish_all(stored)


def force_sums(
    order, partners, columns, right, left, weights, square, slope_high, slope_low, total, store
):
    count = len(columns)
    slots = square.shape[0]
    ahead = slots - 1

    def product(c, n, size):
        square[n % slots, :size, :] = jnp.minimum(jnp.maximum(dot(left[c, :size, :K_ROWS], right[partners[columns[n], c]]), TINY), 4.0)

    def gather(c, n, size):
        w = weights[partners[columns[n], c]]
        return dot(w, slope_high[n % 2, :size, :], LAST) + dot(w, slope_low[n % 2, :size, :], LAST)

    def finish(c):
        found = total[...] + gather(c, count - 1, P_SIZE)
        store(c, found[0:8, :] + found[8:16, :] + found[16:24, :])

    def run(c, before, after, size):
        added = None
        for n in range(count):
            if n + ahead < count:
                product(c, n + ahead, size)
            else:
                product(after, n + ahead - count, P_SIZE)
            if n == 0:
                finish(before)
            else:
                more = gather(c, n - 1, size)
                added = more if n == 1 else added + more
            for base in range(0, size, STEP):
                block = pl.ds(base, STEP)
                s = square[n % slots, block, :]
                y = lax.rsqrt(s)
                q = s * y
                f = (jnp.minimum(y, 1.0) - 1.0) + (jnp.maximum(q, 1.0) - 0.75 * q)
                high = f.astype(bf16)
                slope_high[n % 2, block, :] = high
                slope_low[n % 2, block, :] = (f - high.astype(f32)).astype(bf16)
        total[:, :size] = added

    for n in range(ahead):
        product(cell_at(order, 0), n, P_SIZE)
    by_size(order, run)
    finish(cell_at(order, order.shape[0] - 1))


def near_force_kernel(
    order_ref, rec, rim_lo, rim_hi, left, press_rec, press_lo, press_hi, sums,
    order, copied, table, right, press_table, weights, square, slope_high, slope_low, total,
):
    lists = begin((order_ref, order, copied.at[0]))
    fill_table(table, rec, rim_lo, rim_hi, None, 8)
    fill_table(press_table, press_rec, press_lo, press_hi, None, 2)

    def step(t):
        right[t] = right_operand(table[t], False)
        weights[t] = weight_operand(table[t], press_table[t])

    for_cells(table.shape[0], step)
    finish_all(lists)

    def store(c, found):
        sums[c] = found

    force_sums(
        order, near_partners(rec.shape[0]), list(range(NEAR)), right, left, weights, square, slope_high, slope_low, total, store
    )


def slot_maps(slots, peers):
    block = lax.broadcasted_iota(jnp.int32, (peers, slots), 1) // M
    owner = (block == lax.broadcasted_iota(jnp.int32, (peers, slots), 0)).astype(f32).astype(bf16)
    column = lax.broadcasted_iota(jnp.int32, (slots, HALF), 1)
    slot = lax.broadcasted_iota(jnp.int32, (slots, HALF), 0)
    return owner, column % M == slot % M


def field_map():
    field = lax.broadcasted_iota(jnp.int32, (8, HALF), 1) // M
    return (field == lax.broadcasted_iota(jnp.int32, (8, HALF), 0)).astype(f32)


def force_kernel(
    order_ref, partners_ref, rec, rim_lo, rim_hi, recv, left, press_rec, press_lo, press_hi, press_recv,
    smoothing, pos, vel, press, near, picks,
    state_ref, leaving,
    state, order, partners, copied, table, right, press_table, weights, square, slope_high, slope_low, total, sums,
):
    cells = rec.shape[0]
    lists = begin((order_ref, order, copied.at[0]), (partners_ref, partners, copied.at[1]))
    fill_table(table, rec, rim_lo, rim_hi, recv, 8)
    fill_table(press_table, press_rec, press_lo, press_hi, press_recv, 2)

    def step(t):
        right[t] = right_operand(table[t], False)
        weights[t] = weight_operand(table[t], press_table[t])

    for_cells(table.shape[0], step)
    finish_all(lists)

    def store(c, found):
        found = near[c] + found
        for k in range(8):
            sums[k, pl.ds(c, 1), :] = found[k : k + 1, :]

    force_sums(
        order, partners, list(range(NEAR, partners.shape[0])), right, left, weights, square,
        slope_high, slope_low, total, store,
    )

    width = smoothing[...]
    squared = width * width
    factor = (3.0 * time_step / math.pi) / (squared * squared * width)
    own = press[...]
    live = live_slots(rec)
    for k in range(3):
        place = pos[k]
        centred = place - 0.5
        push = own * (centred * sums[3] - sums[k]) + (centred * sums[7] - sums[4 + k])
        speed = vel[k] + factor * push
        state[k] = jnp.where(live, place + time_step * speed, 0.0)
        state[3 + k] = jnp.where(live, speed, 0.0)

    stored = begin((state, state_ref, copied.at[2]))
    slots = picks.shape[1]
    picked = picks[...]
    chosen = lax.broadcasted_iota(jnp.int32, (P_SIZE, slots), 0) == picked % P_SIZE
    chosen = chosen.astype(f32).astype(bf16)
    mine = lax.broadcasted_iota(jnp.int32, (cells, slots), 0) == picked // P_SIZE
    parts = [split(state[k]) for k in range(6)]
    parts = jnp.concatenate([part[n] for n in range(3) for part in parts], axis=0).astype(bf16)
    found = dot(parts, chosen)
    rows = []
    for k in range(6):
        value = sum(found[(6 * n + k) * cells : (6 * n + k + 1) * cells, :] for n in range(3))
        rows.append(jnp.sum(jnp.where(mine, value, 0.0), axis=0, keepdims=True))
    found = jnp.concatenate(rows + [jnp.zeros((2, slots), f32)], axis=0)
    owner, same = slot_maps(slots, leaving.shape[0])
    spread = field_map()
    blank = jnp.zeros_like(spread)
    spread = jnp.concatenate(
        [jnp.concatenate([spread if n == k else blank for n in range(3)], axis=1) for k in range(3)], axis=0
    )
    wide = dot(jnp.concatenate(split(found), axis=0).astype(bf16), spread.astype(bf16), FIRST)
    wide = jnp.concatenate(
        [jnp.where(same, wide[:, HALF * n : HALF * (n + 1)], 0.0) for n in range(3)], axis=1
    )
    value = dot(owner, wide.astype(bf16))
    leaving[...] = sum(value[:, HALF * n : HALF * (n + 1)] for n in range(3))
    finish_all(stored)


def arrive_kernel(arrived, out):
    owner, same = slot_maps(out.shape[1], arrived.shape[0])
    wide = dot(owner, jnp.concatenate(split(arrived[...]), axis=1).astype(bf16), FIRST)
    wide = jnp.concatenate(
        [jnp.where(same, wide[:, HALF * n : HALF * (n + 1)], 0.0) for n in range(3)], axis=1
    )
    spread = field_map()
    value = dot(jnp.concatenate([spread] * 3, axis=1).astype(bf16), wide.astype(bf16), LAST)
    out[...] = value[: out.shape[0], :]


def call(kernel, outs, smem, hbm, vmem, scratch=(), limit=48, direct=()):
    return pl.pallas_call(
        kernel,
        out_shape=tuple(outs),
        in_specs=[SMEM] * len(smem) + [HBM] * len(hbm) + [VMEM] * len(vmem),
        out_specs=tuple(
            HBM if n in direct else SMEM if out.dtype == jnp.int32 else VMEM for n, out in enumerate(outs)
        ),
        scratch_shapes=scratch,
        compiler_params=pltpu.CompilerParams(vmem_limit_bytes=limit * 1024 * 1024),
    )(*smem, *hbm, *vmem)


def to_neighbours(first, last, axis):
    count = lax.axis_size(axis)
    up = [(i, (i + 1) % count) for i in range(count)]
    down = [(j, i) for i, j in up]
    return lax.ppermute(last, axis, up), lax.ppermute(first, axis, down)


def exchange(value):
    return lax.all_to_all(value, "sub", split_axis=0, concat_axis=0, tiled=True)


def on_device(
    positions, velocities, mass, smoothing, energy, cell_counts, send_cells, partners, mig_list, mig_counts
):
    cells = mass.shape[0]
    peers = lax.axis_size("sub")
    kept = send_cells.shape[2]
    near_width = cells + 2
    full_width = near_width + peers * kept
    send = send_cells[0].T
    links = partners.T

    rec, first, last, outgoing = call(
        pack_kernel,
        [
            shape(cells, 8, HALF),
            shape(1, 8, HALF),
            shape(1, 8, HALF),
            shape(peers, 8 * kept, HALF),
        ],
        [cell_counts, send],
        [],
        [positions, mass],
        limit=60,
    )
    recv = exchange(outgoing)
    rim_lo, rim_hi = to_neighbours(first, last, "slab")

    keep = jnp.arange(M)[None, :] < mig_counts[0][:, None]
    picks = jnp.where(keep, mig_list[0], -P_SIZE).reshape(1, peers * M)

    def tables(width):
        return [
            pltpu.VMEM((width, 8, HALF), f32),
            pltpu.VMEM((width, K_ROWS, P_SIZE), bf16),
        ]

    def sums(size):
        return [
            pltpu.VMEM((size, P_SIZE, P_SIZE), f32),
            pltpu.VMEM((P_SIZE, HALF), f32),
            pltpu.VMEM((P_SIZE, HALF), f32),
            pltpu.VMEM((P_SIZE, HALF), bf16),
            pltpu.VMEM((P_SIZE, HALF), bf16),
        ]

    left, own, order = call(
        operands_kernel,
        [
            jax.ShapeDtypeStruct((cells, P_SIZE, HALF), bf16),
            jax.ShapeDtypeStruct((cells, K_ROWS, P_SIZE), bf16),
            jax.ShapeDtypeStruct((cells,), jnp.int32),
        ],
        [],
        [cell_counts, send],
        [rec, smoothing],
        [pltpu.SMEM((cells,), jnp.int32), pltpu.SemaphoreType.DMA((1,))],
    )
    (near,) = call(
        near_density_kernel,
        [shape(cells, P_SIZE)],
        [],
        [order],
        [rec, rim_lo, rim_hi, left, own],
        [pltpu.SMEM((cells,), jnp.int32), pltpu.SemaphoreType.DMA((1,))] + tables(2) + sums(1),
    )
    density, press, press_rec, first, last, press_out = call(
        density_kernel,
        [
            shape(cells, P_SIZE),
            shape(cells, P_SIZE),
            shape(cells, 2, HALF),
            shape(1, 2, HALF),
            shape(1, 2, HALF),
            shape(peers, 2 * kept, HALF),
        ],
        [],
        [order, links, send],
        [rec, rim_lo, rim_hi, recv, left, smoothing, energy, near],
        tables(full_width)
        + [pltpu.VMEM((cells, P_SIZE), f32), pltpu.VMEM((cells, P_SIZE), f32)]
        + [pltpu.SMEM((cells,), jnp.int32), pltpu.SMEM(links.shape, jnp.int32), pltpu.SMEM(send.shape, jnp.int32)]
        + [pltpu.SemaphoreType.DMA((4,))]
        + sums(2),
        direct=(0,),
    )
    press_recv = exchange(press_out)
    press_lo, press_hi = to_neighbours(first, last, "slab")

    def force_tables(width, slots):
        return tables(width) + [
            pltpu.VMEM((width, 2, HALF), f32),
            pltpu.VMEM((width, V_ROWS, P_SIZE), bf16),
            pltpu.VMEM((slots, P_SIZE, P_SIZE), f32),
            pltpu.VMEM((2, P_SIZE, P_SIZE), bf16),
            pltpu.VMEM((2, P_SIZE, P_SIZE), bf16),
            pltpu.VMEM((V_ROWS, P_SIZE), f32),
        ]

    (near,) = call(
        near_force_kernel,
        [shape(cells, 8, P_SIZE)],
        [],
        [order],
        [rec, rim_lo, rim_hi, left, press_rec, press_lo, press_hi],
        [pltpu.SMEM((cells,), jnp.int32), pltpu.SemaphoreType.DMA((1,))] + force_tables(near_width, 2),
    )
    state, leaving = call(
        force_kernel,
        [shape(6, cells, P_SIZE), shape(peers, HALF)],
        [],
        [order, links],
        [
            rec, rim_lo, rim_hi, recv, left, press_rec, press_lo, press_hi, press_recv,
            smoothing, positions, velocities, press, near, picks,
        ],
        [pltpu.VMEM((6, cells, P_SIZE), f32), pltpu.SMEM((cells,), jnp.int32), pltpu.SMEM(links.shape, jnp.int32)]
        + [pltpu.SemaphoreType.DMA((3,))]
        + force_tables(full_width, 3)
        + [pltpu.VMEM((8, cells, P_SIZE), f32)],
        direct=(0,),
    )
    arrived = exchange(leaving.reshape(peers, 1, HALF)).reshape(peers, HALF)
    (arrivals,) = call(arrive_kernel, [shape(6, peers * M)], [], [], [arrived])
    return density, state, arrivals


def solution(mesh):
    both = ("slab", "sub")
    return jax.shard_map(
        on_device,
        mesh=mesh,
        in_specs=(
            P(None, both, None),
            P(None, both, None),
            P(both, None),
            P(both, None),
            P(both, None),
            P(both),
            P(both, None, None),
            P(both, None),
            P(both, None, None),
            P(both, None),
        ),
        out_specs=(P(both, None), P(None, both, None), P(None, both)),
        check_vma=False,
    )
```
